32 devices in a mesh: sub: 8 (over y, x, core), grp: 4 (over z).
Axes of the slice: x: 2, y: 2, z: 4, core: 2. Of those that a mesh axis runs over, the one named last changes fastest.
Arguments:
- forces: float32 [8, 4, 750, 128], P('sub', 'grp'), may hold values from -52 to 52
- stiffness: bfloat16 [375, 375], replicated, may hold values from -0.0108443534 to 0.61, as said below
- local_solve: bfloat16 [375, 375], replicated, may hold values from -0.01600833 to 0.91, as said below
- moduli: float32 [8, 4, 4], P('sub', 'grp'), may hold values from 0.25 to 2.5
- coarse_basis: float32 [8, 4, 750], P('sub', 'grp'), may hold values from -0.21875 to 0.21875
- coarse_inverse: float32 [32, 32], P(('sub', 'grp')), may hold values from -2.4206146 to 41.079192, as said below
- send_index: int32 [8, 4, 4, 316], P('sub', 'grp'), may hold values from 0 to 1500, as said below
- owner_slot: int32 [8, 4, 4, 316], P('sub', 'grp'), may hold values from 0 to 750, as said below
- home_slot: int32 [8, 4, 1500], P('sub', 'grp'), may hold values from 0 to 750, as said below
Outputs:
- solution: float32 [8, 4, 750, 128], P('sub', 'grp')
- residual: float32 [8, 4, 750, 128], P('sub', 'grp')
The draws below stay inside these ranges and needn't reach their ends.
Inputs may be any that keep to these rules, and one draw needn't show every extreme that they name: For each subdomain and each member j of its slab, the used slots of the message to j (send_index below 1500) come first and unused ones hold 1500. Each subdomain sends to exactly 2 other members of its slab, every such message has used slots, and the relation is symmetric; all other messages, the one to itself included, are unused. Local degrees of freedom below 750 are never sent; exactly 562 local degrees of freedom of each subdomain are sent, each in exactly one used slot; on every subdomain one message has all 316 slots used. owner_slot[s, j, i, k] is below 750 exactly where send_index[s, i, j, k] is a used slot and equals 750 elsewhere. home_slot[s, i, l] equals 750 exactly where local degree of freedom l of subdomain (s, i) is sent; every owned degree of freedom of a subdomain is read by at least one of its local degrees of freedom that are not sent. `stiffness`: symmetric positive definite. `local_solve`: symmetric positive definite. `coarse_inverse`: symmetric positive definite.
All inputs are finite; a program needn't handle non-finite values.
Results may differ from the reference program's by a relative error of at most 0.0053.
Values may be sent and summed in bfloat16 or wider, within the bound.
No kernel may reach another device: no remote copies, remote signals or barrier semaphores. Data moves between devices by JAX's collectives and lax.ppermute only.
A program may use at most 64 MiB of HBM per device.

```python
import math
import jax
import jax.numpy as jnp
from jax import lax

ELEMS = 4
NB = 375
LOADS = 128
ITERS = 2
SLABS = 8
GROUP = 4
LOCAL = 1500
OWNED = 750
SENT = 562
NEIGH = 2
CAP = 316
COARSE = 32


def definite_matrix(key, order_size, diag_low):
    key_one = jax.random.fold_in(key, 0)
    key_three = jax.random.fold_in(key, 2)
    reach_span = 0.5 * diag_low / math.sqrt(order_size)
    raw_values = jax.random.uniform(key_one, (order_size, order_size), jnp.float32, -reach_span, reach_span)
    upper_part = jnp.triu(raw_values, 1)
    diagonal = jax.random.uniform(key_three, (order_size,), jnp.float32, diag_low, 1.5 * diag_low)
    return upper_part + upper_part.T + jnp.diag(diagonal)


def draw_stiffness(key, part):
    matrix = definite_matrix(jax.random.fold_in(key, 1), NB, 0.4)
    return matrix.astype(jnp.bfloat16)


def draw_local_solve(key, part):
    matrix = definite_matrix(jax.random.fold_in(key, 2), NB, 0.6)
    return matrix.astype(jnp.bfloat16)


def draw_coarse_inverse(key, part):
    root_owned = OWNED ** 0.5
    matrix = definite_matrix(jax.random.fold_in(key, 3), COARSE, root_owned)
    return matrix


def draw_forces(key, part):
    key_one, key_two = jax.random.split(jax.random.fold_in(key, 4), 2)
    field_shape = (SLABS, GROUP, OWNED, LOADS)
    device = (jnp.arange(SLABS)[:, None] * GROUP + jnp.arange(GROUP)[None, :]).astype(jnp.float32)
    device_ramp = device / max(SLABS * GROUP - 1, 1)
    row_scale = 0.3 * jnp.exp(jax.random.uniform(key_two, (SLABS, GROUP, OWNED, 1), jnp.float32, 0.0, math.log(10.0)))
    spread = (1.0 + 2.0 * device_ramp)[:, :, None, None]
    values = jnp.clip(jax.random.normal(key_one, field_shape, jnp.float32), -4.0, 4.0)
    return values * row_scale * spread


def group_order(single_key):
    return jax.random.permutation(single_key, GROUP).astype(jnp.int32)


def invert_order(order_values):
    return jnp.zeros((GROUP,), jnp.int32).at[order_values].set(jnp.arange(GROUP, dtype=jnp.int32))


def border_order(single_key):
    border = LOCAL - ELEMS // 2 * NB
    return jax.random.permutation(single_key, border).astype(jnp.int32) + (LOCAL - border)


def one_home(sent_rows, visit_key, owned_key, spare_key):
    sent_mask = jnp.zeros((LOCAL,), jnp.int32).at[sent_rows].set(1)
    visit_order = jax.random.permutation(visit_key, LOCAL).astype(jnp.int32)
    kept_rows = 1 - jnp.take(sent_mask, visit_order)
    home_rank = jnp.cumsum(kept_rows) - 1
    owned_order = jax.random.permutation(owned_key, OWNED).astype(jnp.int32)
    spare_rows = jax.random.randint(spare_key, (LOCAL,), 0, OWNED)
    chosen_rows = jnp.where(home_rank < OWNED, jnp.take(owned_order, jnp.clip(home_rank, 0, OWNED - 1)), spare_rows)
    chosen_rows = jnp.where(kept_rows == 1, chosen_rows, OWNED).astype(jnp.int32)
    return jnp.zeros((LOCAL,), jnp.int32).at[visit_order].set(chosen_rows)


def routing(key):
    base_count = SENT // NEIGH
    eighth = base_count // 8
    extra_slots = SENT % NEIGH
    reach_count = NEIGH // 2
    key_list = jax.random.split(jax.random.fold_in(key, 11), 9)
    placed = jax.vmap(group_order)(jax.random.split(key_list[0], SLABS))
    holder = jax.vmap(invert_order)(placed)
    offsets = jnp.arange(1, reach_count + 1, dtype=jnp.int32)
    ahead_place = (placed[:, :, None] + offsets[None, None, :]) % GROUP
    behind_place = (placed[:, :, None] - offsets[None, None, :] + GROUP) % GROUP
    ahead_member = jnp.take_along_axis(holder, ahead_place.reshape(SLABS, GROUP * reach_count), axis=1)
    ahead_member = ahead_member.reshape(SLABS, GROUP, reach_count)
    behind_member = jnp.take_along_axis(holder, behind_place.reshape(SLABS, GROUP * reach_count), axis=1)
    behind_member = behind_member.reshape(SLABS, GROUP, reach_count)
    swing_size = jax.random.randint(key_list[1], (SLABS, GROUP, reach_count), -eighth, eighth + 1)
    forced = jax.random.randint(key_list[2], (SLABS, GROUP, 1), 0, reach_count)
    flipped = jax.random.randint(key_list[3], (SLABS, GROUP, 1), 0, 2)
    chosen = jnp.arange(reach_count)[None, None, :] == forced
    swing_size = jnp.where(chosen, jnp.where(flipped == 1, -eighth, eighth), swing_size)
    ahead_count = base_count + swing_size + jnp.where(chosen & (flipped == 0), extra_slots, 0)
    behind_count = base_count - swing_size + jnp.where(chosen & (flipped == 1), extra_slots, 0)
    members = jnp.arange(GROUP, dtype=jnp.int32)
    counts = jnp.sum((ahead_member[..., None] == members) * ahead_count[..., None], axis=2)
    counts = counts + jnp.sum((behind_member[..., None] == members) * behind_count[..., None], axis=2)
    counts = counts.astype(jnp.int32)
    starts = jnp.cumsum(counts, axis=-1) - counts
    boundary = jax.vmap(border_order)(jax.random.split(key_list[4], SLABS * GROUP))
    boundary = boundary.reshape(SLABS, GROUP, LOCAL - ELEMS // 2 * NB)
    slot_ids = jnp.arange(CAP, dtype=jnp.int32)[None, None, None, :]
    live_slots = slot_ids < counts[..., None]
    where_from = jnp.minimum(starts[..., None] + slot_ids, SENT - 1)
    picked = jnp.take_along_axis(boundary, where_from.reshape(SLABS, GROUP, GROUP * CAP), axis=2)
    picked = picked.reshape(SLABS, GROUP, GROUP, CAP)
    send_index = jnp.where(live_slots, picked, LOCAL).astype(jnp.int32)
    live_owner = jnp.swapaxes(live_slots, 1, 2)
    owned_pick = jax.random.randint(key_list[5], (SLABS, GROUP, GROUP, CAP), 0, OWNED)
    owner_slot = jnp.where(live_owner, owned_pick, OWNED).astype(jnp.int32)
    sent_rows = boundary[:, :, :SENT].reshape(SLABS * GROUP, SENT)
    home_slot = jax.vmap(one_home)(sent_rows, jax.random.split(key_list[6], SLABS * GROUP), jax.random.split(key_list[7], SLABS * GROUP), jax.random.split(key_list[8], SLABS * GROUP))
    home_slot = home_slot.reshape(SLABS, GROUP, LOCAL).astype(jnp.int32)
    return (send_index, owner_slot, home_slot)


def draw_send_index(key, part):
    return routing(key)[0]


def draw_owner_slot(key, part):
    return routing(key)[1]


def draw_home_slot(key, part):
    return routing(key)[2]


def level_of(key, extent, cuts, low, high):
    factor_of, own = 1.0, jax.random.fold_in(key, 6)
    for axis_at, shards_of in cuts:
        draws = jnp.exp(jax.random.uniform(jax.random.fold_in(own, axis_at), (shards_of,), jnp.float32, low / len(cuts), high / len(cuts)))
        factor_of = factor_of * jnp.repeat(draws, extent[axis_at] // shards_of).reshape([-1 if axis == axis_at else 1 for axis in range(len(extent))])
    return factor_of


def scatter_about(key, extent, width, bound, shards=(), kind=jnp.bfloat16):
    level = level_of(key, extent, shards, -0.22, 0.18) if shards else 1.0
    drawn = jax.random.normal(key, extent, jnp.float32) * width * level
    return jnp.minimum(jnp.maximum(drawn, -bound), bound).astype(kind)


def setup_inputs(seed: int = 0) -> dict:
    keys = jax.random.split(jax.random.key(seed), 10)
    forces = draw_forces(jax.random.fold_in(keys[9], 71), 0)
    stiffness = draw_stiffness(jax.random.fold_in(keys[9], 71), 0)
    local_solve = draw_local_solve(jax.random.fold_in(keys[9], 71), 0)
    moduli = jnp.clip(jnp.exp(math.log(2.5) - 2.3025851 * jax.random.uniform(keys[3], (SLABS, GROUP, ELEMS), jnp.float32) ** level_of(keys[3], (SLABS, GROUP, ELEMS), ((0, 8), (1, 4)), -0.2, 0.2)), 0.25, 2.5)
    coarse_basis = scatter_about(keys[4], (SLABS, GROUP, OWNED), OWNED ** -0.5, 0.21875, ((0, 8), (1, 4)), jnp.float32)
    coarse_inverse = draw_coarse_inverse(jax.random.fold_in(keys[9], 71), 0)
    send_index = draw_send_index(jax.random.fold_in(keys[9], 71), 0)
    owner_slot = draw_owner_slot(jax.random.fold_in(keys[9], 71), 0)
    home_slot = draw_home_slot(jax.random.fold_in(keys[9], 71), 0)
    return {"forces": forces, "stiffness": stiffness, "local_solve": local_solve, "moduli": moduli, "coarse_basis": coarse_basis, "coarse_inverse": coarse_inverse, "send_index": send_index, "owner_slot": owner_slot, "home_slot": home_slot}


def local_tables(send_index, owner_slot, home_slot):
    facing = jnp.swapaxes(owner_slot, 1, 2)
    peer_ids = lax.broadcasted_iota(jnp.int32, send_index.shape, 2)
    member = lax.broadcasted_iota(jnp.int32, send_index.shape, 1)
    slab_ids = lax.broadcasted_iota(jnp.int32, send_index.shape, 0)
    target = (peer_ids * OWNED + facing).astype(jnp.int32)
    home_member = lax.broadcasted_iota(jnp.int32, home_slot.shape, 1)
    lookup_table = (home_member * OWNED + home_slot).astype(jnp.int32)
    spare_column = jnp.zeros((home_slot.shape[0], home_slot.shape[1], 1), jnp.int32)
    lookup_table = jnp.concatenate([lookup_table, spare_column], axis=2)
    lookup_table = lookup_table.at[slab_ids, member, send_index].set(target)
    return lookup_table[:, :, :LOCAL]


def element_images(field, mapping, moduli, matrix, divide):
    members = field.shape[0]
    columns = field.shape[2]
    flat_field = field.reshape(members * OWNED, columns)
    copies = jnp.take(flat_field, mapping, axis=0).astype(jnp.bfloat16)
    blocks = lax.optimization_barrier(copies).astype(jnp.float32).reshape(members, ELEMS, NB, columns)
    product = jnp.einsum("ab,gebr->gear", matrix.astype(jnp.float32), blocks)
    factor = moduli[:, :, None, None]
    if divide:
        scaled = product / factor
    else:
        scaled = product * factor
    rounded = lax.optimization_barrier(scaled.astype(jnp.bfloat16))
    element_terms = rounded.astype(jnp.float32).reshape(members * LOCAL, columns)
    summed = jnp.zeros_like(flat_field).at[mapping.reshape(-1)].add(element_terms)
    return summed.reshape(field.shape)


def inner_sums(first_field, second_field):
    return jnp.sum(first_field * second_field, axis=(0, 1, 2))


def reference(forces, stiffness, local_solve, moduli, coarse_basis, coarse_inverse, send_index, owner_slot, home_slot):
    mapping = local_tables(send_index, owner_slot, home_slot)

    def apply_blocks(field, matrix, divide):
        def one_slab(packed):
            return element_images(packed[0], packed[1], packed[2], matrix, divide)
        return lax.map(one_slab, (field, mapping, moduli))

    def precondition(residual):
        local_part = apply_blocks(residual, local_solve, True)
        coarse_rows = jnp.einsum("sgo,sgor->sgr", coarse_basis, residual, precision=lax.Precision.HIGHEST)
        coarse_rows = coarse_rows.reshape(COARSE, residual.shape[3])
        answer = jnp.dot(coarse_inverse, coarse_rows, precision=lax.Precision.HIGHEST)
        answer = answer.reshape(residual.shape[0], residual.shape[1], 1, residual.shape[3])
        return local_part + coarse_basis[:, :, :, None] * answer

    solution = jnp.zeros_like(forces)
    residual = forces
    search = precondition(residual)
    direction = search
    weighted = inner_sums(residual, search)
    for iteration in range(ITERS):
        image_field = apply_blocks(direction, stiffness, False)
        step_size = weighted / inner_sums(direction, image_field)
        solution = solution + step_size * direction
        residual = residual - step_size * image_field
        if iteration + 1 < ITERS:
            search = precondition(residual)
            update = inner_sums(residual, search)
            direction = search + (update / weighted) * direction
            weighted = update
    return solution, residual
```

```python
import functools

import jax
import jax.numpy as jnp
from jax import lax
from jax.experimental import pallas as pl
from jax.experimental.pallas import tpu as pltpu
from jax.sharding import PartitionSpec as P

ITERS = 2
LANES = 128
RIDERS = 16


def round_up(value, unit):
    return -(-value // unit) * unit


PLACES = 4


def place_distance(order_ref, place):
    return 0 if place == 0 else order_ref[place - 1]


def slab_kernel(
    order_ref,
    x0_ref,
    x1_ref,
    x2_ref,
    x3_ref,
    t0_ref,
    t1_ref,
    t2_ref,
    t3_ref,
    coarse_ref,
    inverse_ref,
    matrices_ref,
    basis_ref,
    fields_ref,
    images_ref,
    gram_ref,
    tables,
    slots,
    sources,
    sources_t,
    pick,
    put,
    values,
    terms,
    own,
    riders,
    factors,
    square,
):
    owned = values.shape[3]
    half = pick.shape[2]
    block = matrices_ref.shape[1]
    loads = fields_ref.shape[1]
    slot_count = slots.shape[1]
    f32, bf16 = jnp.float32, jnp.bfloat16
    distance = [place_distance(order_ref, place) for place in range(PLACES)]

    for at, (x_ref, t_ref) in enumerate(
        ((x0_ref, t0_ref), (x1_ref, t1_ref), (x2_ref, t2_ref), (x3_ref, t3_ref))
    ):
        terms[0, at] = x_ref[...]
        tables[at] = t_ref[...]
    row_ids = lax.broadcasted_iota(jnp.int32, (RIDERS, owned), 0)
    sources[...] = jnp.full(sources.shape, -1.0, f32)
    slots[...] = jnp.full(slots.shape, -1.0, f32)
    for place in range(PLACES):
        table = tables[distance[place]]
        values[0, place] = terms[0, distance[place]]
        riders[place] = jnp.where(
            row_ids == place, values[0, place, loads : loads + 1, :].astype(f32), 0.0
        ).astype(bf16)
        factors[0, place] = table[6:8, :]
        factors[1, place] = 1.0 / table[6:8, :]
        sources[place : place + 1, :] = table[0:1, :]
        sources[PLACES + place : PLACES + place + 1, :] = table[1:2, :]

    pairs = [(a, (a + step) % PLACES) for step in (1, PLACES - 1) for a in range(PLACES)]
    for pair, (reader, owner) in enumerate(pairs):
        row = pl.ds(2 + (distance[reader] ^ distance[owner]), 1)
        slots[2 * pair : 2 * pair + 1, :] = tables[distance[reader], row, :slot_count]
        slots[2 * pair + 1 : 2 * pair + 2, :] = tables[distance[owner], row, slot_count:]
    slots_t = slots[...].T
    half_ids = lax.broadcasted_iota(jnp.int32, (LANES, half), 1).astype(f32)
    for pair in range(len(pairs)):
        found = jnp.zeros((1, half), f32)
        for start in range(0, slot_count, LANES):
            sent = slots_t[start : start + LANES, 2 * pair : 2 * pair + 1]
            target = slots_t[start : start + LANES, 2 * pair + 1 : 2 * pair + 2] + 1.0
            found = found + jnp.sum(
                jnp.where(half_ids == sent, target, 0.0), axis=0, keepdims=True
            )
        sources[2 * PLACES + pair : 2 * PLACES + pair + 1, :] = found - 1.0
    sources_t[...] = sources[...].T

    chunk = 256
    lane_ids = lax.broadcasted_iota(jnp.int32, (chunk, owned), 1).astype(f32)
    deep_ids = lax.broadcasted_iota(jnp.int32, (chunk, half), 0).astype(f32)
    column_ids = lax.broadcasted_iota(jnp.int32, (chunk, LANES), 1)

    def build(n, carry):
        source = sources[pl.ds(n, 1), :]
        for start in range(0, owned, chunk):
            pick[n, start : start + chunk, :] = jnp.where(
                deep_ids == source - float(start), 1.0, 0.0
            ).astype(bf16)
        for start in range(0, half, chunk):
            column = jnp.sum(
                jnp.where(column_ids == n, sources_t[start : start + chunk, :], 0.0),
                axis=1,
                keepdims=True,
            )
            put[n, start : start + chunk, :] = jnp.where(lane_ids == column, 1.0, 0.0).astype(bf16)
        return carry

    lax.fori_loop(0, 4 * PLACES, build, 0)

    def multiply(left, right):
        return jnp.dot(left, right, preferred_element_type=f32)

    def element(which, place, part, copies):
        rounded = copies.astype(bf16)
        for start in range(0, half, block):
            product = multiply(rounded[:, start : start + block], matrices_ref[which])
            scale = factors[which, place, part : part + 1, start : start + block]
            terms[part, place, :, start : start + block] = (product * scale).astype(bf16)

    def around(place, step):
        return lax.rem(place + step, PLACES)

    def inner(which, source, place):
        element(which, place, 0, multiply(values[source, place], pick[place]))

    def outer(which, source, place):
        ahead, behind = around(place, 1), around(place, PLACES - 1)
        copies = (
            multiply(values[source, place], pick[PLACES + place])
            + multiply(values[source, ahead], pick[2 * PLACES + place])
            + multiply(values[source, behind], pick[3 * PLACES + place])
        )
        element(which, place, 1, copies)

    def collect(place):
        ahead, behind = around(place, 1), around(place, PLACES - 1)
        return (
            multiply(terms[0, place], put[place])
            + multiply(terms[1, place], put[PLACES + place])
            + multiply(terms[1, behind], put[2 * PLACES + behind])
            + multiply(terms[1, ahead], put[3 * PLACES + ahead])
        )

    def stage(at, carry):
        which = lax.rem(at + 1, 2)
        source, target = lax.rem(at, 2), lax.rem(at + 1, 2)

        def spread(place, inside):
            inner(which, source, place)
            outer(which, source, place)
            return inside

        def gather(place, inside):
            summed = collect(place)
            values[target, place] = summed.astype(bf16)

            @pl.when(place == 0)
            def _():
                own[at] = summed

            return inside

        lax.fori_loop(0, PLACES, spread, 0)
        lax.fori_loop(0, PLACES, gather, 0)

        @pl.when(at == 0)
        def _():
            for place in range(PLACES):
                values[1, place, loads:, :] = riders[place]

        return carry

    lax.fori_loop(0, 3, stage, 0)
    inner(0, 1, 0)
    outer(0, 1, 0)
    outer(0, 1, 1)
    outer(0, 1, 3)
    own[3] = collect(0)

    first = order_ref[4] * PLACES
    member = order_ref[3]
    square[...] = jnp.zeros_like(square)
    for place in range(PLACES):
        square[place : place + 1, : inverse_ref.shape[1]] = inverse_ref[
            pl.ds(first + (member ^ distance[place]), 1), :
        ]
    answer = jnp.dot(
        square[0:8, : inverse_ref.shape[1]],
        coarse_ref[...],
        precision=lax.Precision.HIGHEST,
        preferred_element_type=f32,
    )
    square[...] = jnp.zeros_like(square)
    square[0:8, :] = answer
    answer_t = square[...].T
    basis = basis_ref[...]
    start_field = own[0, :loads, :] + answer_t[:, 0:1] * basis
    start_image = own[1, :loads, :]
    next_field = own[2, :loads, :]
    next_image = own[3, :loads, :]
    for place in range(PLACES):
        column = answer_t[:, place : place + 1]
        row = loads + place
        start_image = start_image + column * own[1, row : row + 1, :]
        next_field = next_field + column * own[2, row : row + 1, :]
        next_image = next_image + column * own[3, row : row + 1, :]
    fields_ref[0] = start_field
    fields_ref[1] = next_field
    fields_ref[2] = start_image
    fields_ref[3] = next_image
    images_ref[...] = own[1, loads : loads + 8, :]
    residual = x0_ref[:loads, :].astype(f32)
    lanes = lax.broadcasted_iota(jnp.int32, square.shape, 1)
    collected = jnp.zeros(square.shape, f32)
    for at, product in enumerate(
        (
            residual * start_field,
            start_field * start_image,
            start_image * next_field,
            next_field * next_image,
            basis * start_image,
            basis * next_image,
        )
    ):
        total = jnp.sum(product, axis=1, keepdims=True)
        collected = jnp.where(lanes == at, total, collected)
    gram = collected.T[0:8, :]
    row_at = lax.broadcasted_iota(jnp.int32, gram.shape, 0)
    lane_at = lax.broadcasted_iota(jnp.int32, gram.shape, 1)
    for place in range(PLACES):
        entry = jnp.sum(
            basis * own[1, loads + place : loads + place + 1, :], axis=1, keepdims=True
        )
        here = (row_at == 6) & (lane_at == first + (member ^ distance[place]))
        gram = jnp.where(here, entry, gram)
    gram_ref[...] = gram


def finish_kernel(
    order_ref,
    gram_ref,
    inverse_ref,
    fields_ref,
    images_ref,
    basis_ref,
    forces_ref,
    solution_ref,
    residual_ref,
    answer,
    square,
):
    f32 = jnp.float32
    count = inverse_ref.shape[0]
    owned = forces_ref.shape[0]
    first = order_ref[4] * PLACES
    member = order_ref[3]
    precise = functools.partial(
        jnp.dot, precision=lax.Precision.HIGHEST, preferred_element_type=f32
    )
    coarse = gram_ref[:, 4, :]
    answer[...] = precise(inverse_ref[...], coarse)
    answers = answer[...]
    mixed = precise(gram_ref[:, 6, :count], answers)
    sums = jnp.sum(gram_ref[...], axis=0)
    weighted, curvature = sums[0:1, :], sums[1:2, :]
    cross = sums[2:3, :] + jnp.sum(coarse * answers, axis=0, keepdims=True)
    last = sums[3:4, :] + jnp.sum(
        answers * (2.0 * gram_ref[:, 5, :] + mixed), axis=0, keepdims=True
    )
    step = weighted / curvature
    update = step * step * cross - weighted
    grown = 1.0 + update / weighted
    curvature = grown * grown * curvature - 2.0 * step * grown * cross + step * step * last
    second = update / curvature
    whole = step + second * grown
    back = step * second
    square[...] = jnp.zeros_like(square)
    square[0:1, :] = whole
    square[1:2, :] = back
    for place in range(PLACES):
        at = first + (member ^ place_distance(order_ref, place))
        square[2 + place : 3 + place, :] = back * answer[pl.ds(at, 1), :]
    columns = square[...].T
    whole, back = columns[:, 0:1], columns[:, 1:2]
    for start in range(0, basis_ref.shape[1], LANES):
        part = slice(start, start + LANES)
        size = min(LANES, owned - start)
        iterate = (
            whole * fields_ref[0, :, part]
            - back * fields_ref[1, :, part]
            - columns[:, 2:3] * basis_ref[:, part]
        )
        change = back * fields_ref[3, :, part] - whole * fields_ref[2, :, part]
        for place in range(PLACES):
            change = (
                change + columns[:, 2 + place : 3 + place] * images_ref[place : place + 1, part]
            )
        rows = slice(start, start + size)
        solution_ref[rows, :] = iterate.T[:size]
        residual_ref[rows, :] = forces_ref[rows, :] + change.T[:size]


def slab_body(
    mesh_shape,
    forces,
    stiffness,
    local_solve,
    moduli,
    coarse_basis,
    coarse_inverse,
    send_index,
    owner_slot,
    home_slot,
):
    f32, bf16 = jnp.float32, jnp.bfloat16
    axes = ("sub", "grp")
    loaded = forces[0, 0]
    owned_count, loads = loaded.shape
    elements = moduli.shape[2]
    size = stiffness.shape[0]
    local_count = home_slot.shape[2]
    inner_count = elements // 2
    owned_wide = round_up(owned_count, 256)
    block = round_up(size, LANES)
    half = (elements - inner_count) * block
    slot_wide = half // 2
    devices = mesh_shape["sub"] * mesh_shape["grp"]
    slab = lax.axis_index("sub")
    member = lax.axis_index("grp")
    distances = jnp.arange(PLACES, dtype=jnp.int32)

    basis = jnp.pad(coarse_basis[0, 0], (0, owned_wide - owned_count))[None, :]
    turned = jnp.pad(loaded.astype(bf16), ((0, owned_wide - owned_count), (0, 0))).T
    packed = jnp.concatenate(
        [turned, basis.astype(bf16), jnp.zeros((RIDERS - 1, owned_wide), bf16)], axis=0
    )

    own_term = jnp.dot(
        coarse_basis[0, 0][None, :], loaded, precision=lax.Precision.HIGHEST
    )
    inverse_row = jnp.pad(coarse_inverse, ((0, 0), (0, LANES - coarse_inverse.shape[1])))
    shared = jnp.broadcast_to(
        jnp.concatenate([own_term, inverse_row], axis=0)[None], (devices, 2, LANES)
    )

    home = home_slot[0, 0].reshape(elements, size)
    home = jnp.where(home < owned_count, home, -1).astype(f32)
    home = jnp.pad(home, ((0, 0), (0, block - size)), constant_values=-1.0).reshape(2, half)
    sent = jnp.take(send_index[0, 0], member ^ distances, axis=0)
    used = sent[:, 0] < local_count
    column = (sent // size - inner_count) * block + sent % size
    column = jnp.where(sent < local_count, column, -1).astype(f32)
    target = jnp.take(owner_slot[0, 0], member ^ distances, axis=0)
    target = jnp.where(target < owned_count, target, -1).astype(f32)
    spare = ((0, 0), (0, slot_wide - column.shape[1]))
    routes = jnp.concatenate(
        [
            jnp.pad(column, spare, constant_values=-1.0),
            jnp.pad(target, spare, constant_values=-1.0),
        ],
        axis=1,
    )
    modulus = jnp.broadcast_to(moduli[0, 0][:, None], (elements, block)).reshape(2, half)
    table = jnp.concatenate([home, routes, modulus], axis=0)

    opposite = jnp.sum(jnp.where(used | (distances == 0), 0, distances))
    opposite = jnp.clip(opposite, 1, PLACES - 1)
    near = jnp.where(opposite == 1, 2, 1)
    order = jnp.stack(
        [near, opposite, 6 - near - opposite, member, slab, slab, slab, slab]
    ).astype(jnp.int32)

    def swapped(array, distance):
        return lax.ppermute(array, "grp", [(i, i ^ distance) for i in range(PLACES)])

    tables = [table] + [swapped(table, d) for d in range(1, PLACES)]
    fields = [packed] + [swapped(packed, d) for d in range(1, PLACES)]
    shared = lax.all_to_all(shared, axes, split_axis=0, concat_axis=0, tiled=True)
    coarse = shared[:, 0, :]
    inverse = shared[:, 1, :devices]

    widen = ((0, block - size), (0, block - size))
    matrices = jnp.stack([jnp.pad(stiffness, widen), jnp.pad(local_solve, widen)])

    rows = loads + RIDERS
    smem = pl.BlockSpec(memory_space=pltpu.SMEM)
    vmem = pl.BlockSpec(memory_space=pltpu.VMEM)
    results, images, gram = pl.pallas_call(
        slab_kernel,
        out_shape=(
            jax.ShapeDtypeStruct((4, loads, owned_wide), f32),
            jax.ShapeDtypeStruct((8, owned_wide), f32),
            jax.ShapeDtypeStruct((8, LANES), f32),
        ),
        in_specs=[smem] + [vmem] * 12,
        out_specs=(vmem, vmem, vmem),
        scratch_shapes=[
            pltpu.VMEM((PLACES, 8, half), f32),
            pltpu.VMEM((LANES, slot_wide), f32),
            pltpu.VMEM((LANES, half), f32),
            pltpu.VMEM((half, LANES), f32),
            pltpu.VMEM((4 * PLACES, owned_wide, half), bf16),
            pltpu.VMEM((4 * PLACES, half, owned_wide), bf16),
            pltpu.VMEM((2, PLACES, rows, owned_wide), bf16),
            pltpu.VMEM((2, PLACES, rows, half), bf16),
            pltpu.VMEM((4, rows, owned_wide), f32),
            pltpu.VMEM((PLACES, RIDERS, owned_wide), bf16),
            pltpu.VMEM((2, PLACES, 2, half), f32),
            pltpu.VMEM((LANES, LANES), f32),
        ],
        compiler_params=pltpu.CompilerParams(vmem_limit_bytes=58 * 2**20),
        name="slab",
    )(order, *fields, *tables, coarse, inverse, matrices, basis)

    gathered = lax.all_to_all(
        jnp.broadcast_to(gram[None], (devices, 8, LANES)), axes, 0, 0, tiled=True
    )
    iterate, residual = pl.pallas_call(
        finish_kernel,
        out_shape=(jax.ShapeDtypeStruct((owned_count, loads), f32),) * 2,
        in_specs=[smem] + [vmem] * 6,
        out_specs=(vmem, vmem),
        scratch_shapes=[pltpu.VMEM((devices, LANES), f32), pltpu.VMEM((LANES, LANES), f32)],
        compiler_params=pltpu.CompilerParams(vmem_limit_bytes=32 * 2**20),
        name="finish",
    )(order, gathered, inverse, results, images, basis, loaded)
    return (iterate[None, None], residual[None, None])


def spread_owned(values, slot_rows):
    padded = jnp.concatenate([values, jnp.zeros((1, values.shape[1]), values.dtype)], axis=0)
    return jnp.take(padded, slot_rows, axis=0)


def element_block(copies, matrix, factors, divide):
    columns = copies.shape[-1]
    blocks = copies.reshape(factors.shape[0], matrix.shape[0], columns)
    product = jnp.einsum("ab,ebr->ear", matrix, blocks, preferred_element_type=jnp.float32)
    if divide:
        scaled = product / factors[:, None, None]
    else:
        scaled = product * factors[:, None, None]
    return scaled.astype(jnp.bfloat16).reshape(-1, columns)


def exchange_body(
    forces,
    stiffness,
    local_solve,
    moduli,
    coarse_basis,
    coarse_inverse,
    send_index,
    owner_slot,
    home_slot,
):
    loaded = forces[0, 0]
    owned_count = loaded.shape[0]
    send_rows = send_index[0, 0]
    slot_rows = owner_slot[0, 0]
    home_rows = home_slot[0, 0]
    elastic = moduli[0, 0]
    basis_values = coarse_basis[0, 0]
    groups, capacity = send_rows.shape
    block_size = stiffness.shape[0]
    inner_count = elastic.shape[0] // 2
    border_start = inner_count * block_size
    local_count = home_rows.shape[0]
    inner_elastic = elastic[:inner_count]
    outer_elastic = elastic[inner_count:]
    sent_position = (
        jnp.zeros((local_count + 1,), jnp.int32)
        .at[send_rows.reshape(-1)]
        .set(jnp.arange(groups * capacity, dtype=jnp.int32))[:local_count]
    )
    position = jnp.where(home_rows < owned_count, groups * capacity + home_rows, sent_position)
    inner_home = home_rows[:border_start]
    outer_rows = position[border_start:]
    gather_rows = jnp.concatenate([slot_rows.reshape(-1), home_rows], axis=0)
    device = lax.axis_index(("sub", "grp"))
    full_inverse = lax.all_gather(coarse_inverse, ("sub", "grp"), axis=0, tiled=True)

    def joined(received, own_values):
        columns = received.shape[2]
        return jnp.concatenate([received.reshape(-1, columns), own_values], axis=0)

    def return_terms(inner_terms, outer_copies, matrix, divide):
        outer_terms = element_block(outer_copies, matrix, outer_elastic, divide)
        element_terms = jnp.concatenate([inner_terms, outer_terms], axis=0)
        columns = element_terms.shape[1]
        padded = jnp.concatenate(
            [element_terms, jnp.zeros((1, columns), element_terms.dtype)], axis=0
        )
        outgoing = jnp.take(padded, send_rows, axis=0)
        returned = lax.all_to_all(outgoing, "grp", split_axis=0, concat_axis=0, tiled=True)
        contributions = jnp.concatenate(
            [returned.reshape(-1, columns), element_terms], axis=0
        ).astype(jnp.float32)
        summed = (
            jnp.zeros((owned_count + 1, columns), jnp.float32).at[gather_rows].add(contributions)
        )
        return summed[:owned_count]

    def residual_solve(residual):
        own_copy = residual.astype(jnp.bfloat16)
        inner_terms = element_block(
            jnp.take(own_copy, inner_home, axis=0), local_solve, inner_elastic, True
        )
        received = lax.all_to_all(
            spread_owned(own_copy, slot_rows), "grp", split_axis=0, concat_axis=0, tiled=True
        )
        outer_copies = jnp.take(joined(received, own_copy), outer_rows, axis=0)
        return return_terms(inner_terms, outer_copies, local_solve, True)

    def coarse_step(residual, local_part):
        own_term = jnp.dot(basis_values[None, :], residual, precision=lax.Precision.HIGHEST)
        spread = jnp.zeros((full_inverse.shape[0], own_term.shape[1]), jnp.float32)
        spread = lax.dynamic_update_slice(spread, own_term, (device, jnp.int32(0)))
        totals, partial_value = lax.psum(
            (spread, jnp.sum(residual * local_part, axis=0)), ("sub", "grp")
        )
        answer = jnp.dot(full_inverse, totals, precision=lax.Precision.HIGHEST)
        own_answer = lax.dynamic_slice_in_dim(answer, device, 1, 0)
        search = local_part + basis_values[:, None] * own_answer
        weighted = partial_value + jnp.sum(totals * answer, axis=0)
        return (search, weighted)

    solution = jnp.zeros_like(loaded)
    residual = loaded
    local_part = residual_solve(residual)
    search, weighted = coarse_step(residual, local_part)
    direction = search
    for iteration in range(ITERS):
        apply_own_copy = direction.astype(jnp.bfloat16)
        apply_inner_terms = element_block(
            jnp.take(apply_own_copy, inner_home, axis=0), stiffness, inner_elastic, False
        )
        apply_received = lax.all_to_all(
            spread_owned(apply_own_copy, slot_rows), "grp", split_axis=0, concat_axis=0, tiled=True
        )
        apply_outer_copies = jnp.take(joined(apply_received, apply_own_copy), outer_rows, axis=0)
        image_field = return_terms(apply_inner_terms, apply_outer_copies, stiffness, False)
        final_turn = iteration + 1 == ITERS
        curvature = lax.psum(jnp.sum(direction * image_field, axis=0), ("sub", "grp"))
        step_size = weighted / curvature
        solution = solution + step_size[None, :] * direction
        residual = residual - step_size[None, :] * image_field
        if not final_turn:
            local_part = residual_solve(residual)
            search, update = coarse_step(residual, local_part)
            direction = search + (update / weighted)[None, :] * direction
            weighted = update
    return (solution[None, None], residual[None, None])


def solution(mesh):
    if mesh.shape["grp"] == PLACES:
        body = functools.partial(slab_body, dict(mesh.shape))
    else:
        body = exchange_body
    return jax.shard_map(
        body,
        mesh=mesh,
        in_specs=(
            P("sub", "grp", None, None),
            P(),
            P(),
            P("sub", "grp", None),
            P("sub", "grp", None),
            P(("sub", "grp"), None),
            P("sub", "grp", None, None),
            P("sub", "grp", None, None),
            P("sub", "grp", None),
        ),
        out_specs=(P("sub", "grp", None, None), P("sub", "grp", None, None)),
        check_vma=False,
    )
```

```python
import functools

import jax
import jax.numpy as jnp
from jax import lax
from jax.experimental import pallas as pl
from jax.experimental.pallas import tpu as pltpu
from jax.sharding import PartitionSpec as P

ITERS = 2
LANES = 128
RIDERS = 16
PLACES = 4


def round_up(value, unit):
    return -(-value // unit) * unit


def place_distances(order_ref):
    return [0] + [order_ref[place - 1] for place in range(1, PLACES)]


def turn(ref, rows, width):
    return ref[rows : rows + LANES, :width].T


def pack_kernel(
    forces_hbm,
    basis_hbm,
    inverse_hbm,
    send_hbm,
    owner_hbm,
    home_hbm,
    moduli_hbm,
    packed_ref,
    table_ref,
    padded,
    wide_ref,
    basis_ref,
    inverse_ref,
    send_ref,
    owner_ref,
    home_ref,
    moduli_ref,
    square,
    arrived,
):
    f32, bf16 = jnp.float32, jnp.bfloat16
    owned, _, loads = forces_hbm.shape
    wide = padded.shape[0]
    half = table_ref.shape[1]
    members, capacity = send_ref.shape
    local = home_ref.shape[1]
    copies = [
        pltpu.make_async_copy(source, target, arrived.at[at])
        for at, (source, target) in enumerate(
            (
                (forces_hbm.at[:, 0, :], padded.at[:owned, :]),
                (basis_hbm, basis_ref),
                (inverse_hbm, inverse_ref),
                (send_hbm, send_ref),
                (owner_hbm, owner_ref),
                (home_hbm, home_ref),
                (moduli_hbm, moduli_ref),
            )
        )
    ]
    for copy in copies:
        copy.start()
    padded[owned:, :] = jnp.zeros((wide - owned, loads), f32)
    wide_ref[...] = jnp.zeros_like(wide_ref)
    table_ref[...] = jnp.full(table_ref.shape, -1.0, f32)
    for copy in copies:
        copy.wait()
    wide_ref[0:1, :owned] = basis_ref[...]
    basis = wide_ref[0:1, :]
    term = jnp.zeros((loads, 1), f32)
    for start in range(0, wide, LANES):
        turned = padded[start : start + LANES, :].T
        packed_ref[:loads, start : start + LANES] = turned.astype(bf16)
        term = term + jnp.sum(
            turned * basis[:, start : start + LANES], axis=1, keepdims=True
        )
    row_ids = lax.broadcasted_iota(jnp.int32, (RIDERS, wide), 0)
    packed_ref[loads:, :] = jnp.where(row_ids == 0, basis, 0.0).astype(bf16)

    table_ref[0:1, :] = home_ref[:, :half].astype(f32)
    table_ref[1:2, : local - half] = home_ref[:, half:].astype(f32)
    table_ref[2 : 2 + members, :capacity] = send_ref[...].astype(f32)
    table_ref[2 : 2 + members, half // 2 : half // 2 + capacity] = owner_ref[...].astype(f32)
    table_ref[6:7, : moduli_ref.shape[1]] = moduli_ref[...]
    square[...] = jnp.broadcast_to(term, square.shape)
    table_ref[7:8, :] = jnp.zeros((1, half), f32)
    table_ref[7:8, :LANES] = square[...].T[0:1, :]
    table_ref[7:8, LANES : LANES + inverse_ref.shape[1]] = inverse_ref[...]


def build_kernel(
    size,
    owned_count,
    local_count,
    order_ref,
    tables,
    pick0,
    pick1,
    pick2,
    pick3,
    put0,
    put1,
    put2,
    put3,
    factors,
    slots,
    homes,
    sources,
    sources_t,
):
    picks, puts = (pick0, pick1, pick2, pick3), (put0, put1, put2, put3)
    owned, half = pick0.shape[1], pick0.shape[2]
    block = half // 2
    slot_count = slots.shape[1]
    f32, bf16 = jnp.float32, jnp.bfloat16
    distance = place_distances(order_ref)
    member = order_ref[3]
    elements = 4
    sources[...] = jnp.full(sources.shape, -1.0, f32)
    slots[...] = jnp.full(slots.shape, -1.0, f32)
    homes[...] = jnp.zeros_like(homes)
    lane_block = lax.broadcasted_iota(jnp.int32, (8, block), 1)
    for place in range(PLACES):
        homes[place : place + 1, :half] = tables[distance[place], 0:1, :]
        homes[place : place + 1, half:] = tables[distance[place], 1:2, :]
        for e in range(elements):
            modulus = jnp.broadcast_to(tables[distance[place], 6:7, e : e + 1], (1, block))
            factors[0, place, e : e + 1, :] = modulus
            factors[1, place, e : e + 1, :] = 1.0 / modulus

    all_homes = homes[...]
    for e in range(elements):
        shift = (all_homes.shape[1] - e * size) % all_homes.shape[1]
        moved = all_homes if e == 0 else pltpu.roll(all_homes, shift, 1)
        rows = moved[:, :block]
        rows = jnp.where((lane_block < size) & (rows < float(owned_count)), rows, -1.0)
        part, column = e // 2, (e % 2) * block
        sources[part * PLACES : (part + 1) * PLACES, column : column + block] = rows[:PLACES]

    pairs = [(a, (a + step) % PLACES) for step in (1, PLACES - 1) for a in range(PLACES)]
    for pair, (reader, owner) in enumerate(pairs):
        to_owner = pl.ds(2 + (member ^ distance[owner]), 1)
        to_reader = pl.ds(2 + (member ^ distance[reader]), 1)
        sent = tables[distance[reader], to_owner, :slot_count]
        sent = jnp.where(sent < float(local_count), sent, -1.0)
        first = float(2 * size)
        moved = sent - first + jnp.where(sent >= first + size, float(block - size), 0.0)
        slots[2 * pair : 2 * pair + 1, :] = jnp.where(sent < 0.0, -1.0, moved)
        slots[2 * pair + 1 : 2 * pair + 2, :] = tables[distance[owner], to_reader, slot_count:]
    slots_t = slots[...].T
    half_ids = lax.broadcasted_iota(jnp.int32, (LANES, half), 1).astype(f32)
    for pair in range(len(pairs)):
        found = jnp.zeros((1, half), f32)
        for start in range(0, slot_count, LANES):
            column = slots_t[start : start + LANES, 2 * pair : 2 * pair + 1]
            target = slots_t[start : start + LANES, 2 * pair + 1 : 2 * pair + 2] + 1.0
            found = found + jnp.sum(
                jnp.where(half_ids == column, target, 0.0), axis=0, keepdims=True
            )
        sources[2 * PLACES + pair : 2 * PLACES + pair + 1, :] = found - 1.0
    sources_t[...] = sources[...].T

    chunk = 256
    lane_ids = lax.broadcasted_iota(jnp.int32, (chunk, owned), 1).astype(f32)
    deep_ids = lax.broadcasted_iota(jnp.int32, (chunk, half), 0).astype(f32)
    column_ids = lax.broadcasted_iota(jnp.int32, (chunk, LANES), 1)

    for kind, (pick, put) in enumerate(zip(picks, puts)):

        def build(place, carry):
            n = kind * PLACES + place
            source = sources[pl.ds(n, 1), :]
            for start in range(0, owned, chunk):
                pick[place, start : start + chunk, :] = jnp.where(
                    deep_ids == source - float(start), 1.0, 0.0
                ).astype(bf16)
            for start in range(0, half, chunk):
                column = jnp.sum(
                    jnp.where(column_ids == n, sources_t[start : start + chunk, :], 0.0),
                    axis=1,
                    keepdims=True,
                )
                put[place, start : start + chunk, :] = jnp.where(
                    lane_ids == column, 1.0, 0.0
                ).astype(bf16)
            return carry

        lax.fori_loop(0, PLACES, build, 0)


def chain_kernel(
    order_ref,
    x0_ref,
    x1_ref,
    x2_ref,
    x3_ref,
    pick0,
    pick1,
    pick2,
    pick3,
    put0,
    put1,
    put2,
    put3,
    factors,
    matrices_ref,
    own,
    values,
    terms,
    copies,
    riders,
):
    owned, half = pick0.shape[1], pick0.shape[2]
    block = matrices_ref.shape[1]
    rows = own.shape[1]
    loads = rows - RIDERS
    f32, bf16 = jnp.float32, jnp.bfloat16
    distance = place_distances(order_ref)
    for at, x_ref in enumerate((x0_ref, x1_ref, x2_ref, x3_ref)):
        values[1, at] = x_ref[...]
    row_ids = lax.broadcasted_iota(jnp.int32, (RIDERS, owned), 0)
    for place in range(PLACES):
        values[0, place] = values[1, distance[place]]
        riders[place] = jnp.where(
            row_ids == place, values[0, place, loads : loads + 1, :].astype(f32), 0.0
        ).astype(bf16)

    def multiply(left, right):
        return jnp.dot(left, right, preferred_element_type=f32)

    def beside(refs):
        return jnp.concatenate(refs, axis=1)

    def above(refs):
        return jnp.concatenate(refs, axis=0)

    def split(place, part, copied):
        copied = copied.astype(bf16)
        copies[place, 2 * part] = copied[:, :block]
        copies[place, 2 * part + 1] = copied[:, block:]

    def inner(source, place):
        split(place, 0, multiply(values[source, place], pick0[place]))

    def outer(source, place):
        ahead, behind = (place + 1) % PLACES, (place - 1) % PLACES
        fields = beside([values[source, at] for at in (place, ahead, behind)])
        split(place, 1, multiply(fields, above([pick1[place], pick2[place], pick3[place]])))

    def scaled(which, at, count):
        product = multiply(copies[at].reshape(count * 4 * rows, block), matrices_ref[which])
        scale = factors[which, at].reshape(count, 4, 1, block)
        terms[at] = (product.reshape(count, 4, rows, block) * scale).astype(bf16)

    def collect(place):
        ahead, behind = (place + 1) % PLACES, (place - 1) % PLACES
        ends = beside(
            [terms[place, e] for e in range(4)]
            + [terms[behind, 2], terms[behind, 3], terms[ahead, 2], terms[ahead, 3]]
        )
        return multiply(ends, above([put0[place], put1[place], put2[behind], put3[ahead]]))

    def stage(at, carry):
        which = lax.rem(at + 1, 2)
        source, target = lax.rem(at, 2), lax.rem(at + 1, 2)
        for place in range(PLACES):
            inner(source, place)
            outer(source, place)
        scaled(which, slice(0, PLACES), PLACES)
        for place in range(PLACES):
            summed = collect(place)
            values[target, place] = summed.astype(bf16)
            if place == 0:
                own[at] = summed

        @pl.when(at == 0)
        def _():
            for place in range(PLACES):
                values[1, place, loads:, :] = riders[place]

        return carry

    lax.fori_loop(0, 3, stage, 0)
    inner(1, 0)
    outer(1, 0)
    outer(1, 1)
    outer(1, 3)
    scaled(0, slice(0, 2), 2)
    scaled(0, slice(3, 4), 1)
    own[3] = collect(0)


def dots_kernel(
    order_ref,
    own,
    x0_ref,
    shared_ref,
    wide_ref,
    fields_ref,
    gram_ref,
    inverse,
    coarse_ref,
    square,
):
    f32 = jnp.float32
    devices = inverse.shape[0]
    loads = fields_ref.shape[1]
    distance = place_distances(order_ref)
    member = order_ref[3]
    first = order_ref[4] * PLACES
    for at in range(devices // PLACES):
        for apart in range(PLACES):
            row = pl.ds(at * PLACES + (member ^ apart), 1)
            coarse_ref[row, :] = shared_ref[at, apart : apart + 1, :]
            inverse[row, :] = shared_ref[at, PLACES + apart : PLACES + apart + 1, :]
    square[...] = jnp.zeros_like(square)
    for place in range(PLACES):
        square[place : place + 1, :] = inverse[pl.ds(first + (member ^ distance[place]), 1), :]
    answer = jnp.dot(
        square[0:8, :devices],
        coarse_ref[...],
        precision=lax.Precision.HIGHEST,
        preferred_element_type=f32,
    )
    square[...] = jnp.zeros_like(square)
    square[0:8, :] = answer
    answer_t = square[...].T
    basis = wide_ref[0:1, :]
    start_field = own[0, :loads, :] + answer_t[:, 0:1] * basis
    start_image = own[1, :loads, :]
    next_field = own[2, :loads, :]
    next_image = own[3, :loads, :]
    for place in range(PLACES):
        column = answer_t[:, place : place + 1]
        row = loads + place
        start_image = start_image + column * own[1, row : row + 1, :]
        next_field = next_field + column * own[2, row : row + 1, :]
        next_image = next_image + column * own[3, row : row + 1, :]
    fields_ref[0] = start_field
    fields_ref[1] = next_field
    fields_ref[2] = start_image
    fields_ref[3] = next_image
    residual = x0_ref[:loads, :].astype(f32)
    lanes = lax.broadcasted_iota(jnp.int32, square.shape, 1)
    collected = jnp.zeros(square.shape, f32)
    for at, product in enumerate(
        (
            residual * start_field,
            start_field * start_image,
            start_image * next_field,
            next_field * next_image,
            basis * start_image,
            basis * next_image,
        )
    ):
        total = jnp.sum(product, axis=1, keepdims=True)
        collected = jnp.where(lanes == at, total, collected)
    gram = collected.T[0:8, :]
    row_at = lax.broadcasted_iota(jnp.int32, gram.shape, 0)
    lane_at = lax.broadcasted_iota(jnp.int32, gram.shape, 1)
    for place in range(PLACES):
        entry = jnp.sum(
            basis * own[1, loads + place : loads + place + 1, :], axis=1, keepdims=True
        )
        here = (row_at == 6) & (lane_at == first + (member ^ distance[place]))
        gram = jnp.where(here, entry, gram)
    gram_ref[...] = jnp.broadcast_to(gram[None], gram_ref.shape)


def finish_kernel(
    order_ref,
    gram_ref,
    inverse,
    fields_ref,
    own,
    wide_ref,
    padded,
    solution_hbm,
    residual_hbm,
    answer,
    square,
    iterates,
    residuals,
    sent,
):
    f32 = jnp.float32
    count = inverse.shape[0]
    owned, _, loads = solution_hbm.shape
    first = order_ref[4] * PLACES
    member = order_ref[3]
    distance = place_distances(order_ref)
    precise = functools.partial(
        jnp.dot, precision=lax.Precision.HIGHEST, preferred_element_type=f32
    )
    coarse = gram_ref[:, 4, :]
    answer[...] = precise(inverse[:, :count], coarse)
    answers = answer[...]
    mixed = precise(gram_ref[:, 6, :count], answers)
    sums = jnp.sum(gram_ref[...], axis=0)
    weighted, curvature = sums[0:1, :], sums[1:2, :]
    cross = sums[2:3, :] + jnp.sum(coarse * answers, axis=0, keepdims=True)
    last = sums[3:4, :] + jnp.sum(
        answers * (2.0 * gram_ref[:, 5, :] + mixed), axis=0, keepdims=True
    )
    step = weighted / curvature
    update = step * step * cross - weighted
    grown = 1.0 + update / weighted
    curvature = grown * grown * curvature - 2.0 * step * grown * cross + step * step * last
    second = update / curvature
    whole = step + second * grown
    back = step * second
    square[...] = jnp.zeros_like(square)
    square[0:1, :] = whole
    square[1:2, :] = back
    for place in range(PLACES):
        at = first + (member ^ distance[place])
        square[2 + place : 3 + place, :] = back * answer[pl.ds(at, 1), :]
    columns = square[...].T
    whole, back = columns[:, 0:1], columns[:, 1:2]
    copies = []
    for start in range(0, wide_ref.shape[1], LANES):
        part = slice(start, start + LANES)
        size = min(LANES, owned - start)
        iterate = (
            whole * fields_ref[0, :, part]
            - back * fields_ref[1, :, part]
            - columns[:, 2:3] * wide_ref[0:1, part]
        )
        change = back * fields_ref[3, :, part] - whole * fields_ref[2, :, part]
        for place in range(PLACES):
            row = loads + place
            change = change + columns[:, 2 + place : 3 + place] * own[1, row : row + 1, part]
        iterates[start : start + LANES, :] = iterate.T
        residuals[start : start + LANES, :] = padded[start : start + LANES, :] + change.T
        rows = slice(start, start + size)
        for at, (source, target) in enumerate(
            ((iterates, solution_hbm), (residuals, residual_hbm))
        ):
            copy = pltpu.make_async_copy(
                source.at[rows, :], target.at[rows, 0, :], sent.at[at, start // LANES]
            )
            copy.start()
            copies.append(copy)
    for copy in copies:
        copy.wait()


def slab_body(
    mesh_shape,
    forces,
    stiffness,
    local_solve,
    moduli,
    coarse_basis,
    coarse_inverse,
    send_index,
    owner_slot,
    home_slot,
):
    f32, bf16, i32 = jnp.float32, jnp.bfloat16, jnp.int32
    axes = ("sub", "grp")
    owned_count, loads = forces.shape[2:]
    size = stiffness.shape[0]
    local_count = home_slot.shape[2]
    owned_wide = round_up(owned_count, 256)
    block = round_up(size, LANES)
    half = 2 * block
    devices = mesh_shape["sub"] * mesh_shape["grp"]
    rows = loads + RIDERS
    slab = lax.axis_index("sub")
    member = lax.axis_index("grp")
    smem = pl.BlockSpec(memory_space=pltpu.SMEM)
    vmem = pl.BlockSpec(memory_space=pltpu.VMEM)

    anywhere = pl.BlockSpec(memory_space=pltpu.HBM)
    slabs = mesh_shape["sub"]

    packed, table, padded, wide = pl.pallas_call(
        pack_kernel,
        out_shape=(
            jax.ShapeDtypeStruct((rows, owned_wide), bf16),
            jax.ShapeDtypeStruct((8, half), f32),
            jax.ShapeDtypeStruct((owned_wide, loads), f32),
            jax.ShapeDtypeStruct((8, owned_wide), f32),
        ),
        in_specs=[anywhere] * 7,
        out_specs=(vmem,) * 4,
        scratch_shapes=[
            pltpu.VMEM((1, owned_count), f32),
            pltpu.VMEM((1, devices), f32),
            pltpu.VMEM(send_index.shape[2:], i32),
            pltpu.VMEM(owner_slot.shape[2:], i32),
            pltpu.VMEM((1, local_count), i32),
            pltpu.VMEM((1, moduli.shape[2]), f32),
            pltpu.VMEM((LANES, LANES), f32),
            pltpu.SemaphoreType.DMA((7,)),
        ],
        compiler_params=pltpu.CompilerParams(vmem_limit_bytes=62 * 2**20),
        name="pack",
    )(
        forces.reshape(owned_count, 1, loads),
        coarse_basis[0],
        coarse_inverse,
        send_index[0, 0],
        owner_slot[0, 0],
        home_slot[0],
        moduli[0],
    )

    used = send_index[0, 0, :, 0] < local_count
    distances = jnp.arange(PLACES, dtype=i32) ^ member
    opposite = jnp.clip(jnp.sum(jnp.where(used, 0, distances)), 1, PLACES - 1)
    near = jnp.where(opposite == 1, 2, 1)
    order = jnp.stack(
        [
            near,
            opposite,
            6 - near - opposite,
            member,
            slab,
            slab,
            slab,
            slab,
        ]
    ).astype(i32)

    def swapped(array, distance):
        return lax.ppermute(array, "grp", [(i, i ^ distance) for i in range(PLACES)])

    near_table = swapped(table, 1)
    packed, near_table = lax.optimization_barrier((packed, near_table))
    tables = jnp.stack([table, near_table, swapped(table, 2), swapped(table, 3)])
    fields = [packed] + [swapped(packed, d) for d in range(1, PLACES)]
    shared = jnp.concatenate([tables[:, 7, :LANES], tables[:, 7, LANES : 2 * LANES]], axis=0)
    shared = jnp.broadcast_to(shared[None], (slabs, 8, LANES))
    shared = lax.all_to_all(shared, "sub", split_axis=0, concat_axis=0, tiled=True)

    widen = ((0, block - size), (0, block - size))
    matrices = jnp.stack([jnp.pad(stiffness, widen), jnp.pad(local_solve, widen)])

    *choices, factors = pl.pallas_call(
        functools.partial(build_kernel, size, owned_count, local_count),
        out_shape=(
            *[jax.ShapeDtypeStruct((PLACES, owned_wide, half), bf16)] * 4,
            *[jax.ShapeDtypeStruct((PLACES, half, owned_wide), bf16)] * 4,
            jax.ShapeDtypeStruct((2, PLACES, 4, block), f32),
        ),
        in_specs=[smem, vmem],
        out_specs=(vmem,) * 9,
        scratch_shapes=[
            pltpu.VMEM((LANES, half // 2), f32),
            pltpu.VMEM((8, 2 * half), f32),
            pltpu.VMEM((LANES, half), f32),
            pltpu.VMEM((half, LANES), f32),
        ],
        compiler_params=pltpu.CompilerParams(vmem_limit_bytes=8 * 2**20),
        cost_estimate=pl.CostEstimate(
            flops=8 * 10**9, bytes_accessed=38 * 10**6, transcendentals=0
        ),
        name="build",
    )(order, tables)

    own = pl.pallas_call(
        chain_kernel,
        out_shape=jax.ShapeDtypeStruct((4, rows, owned_wide), f32),
        in_specs=[smem] + [vmem] * 14,
        out_specs=vmem,
        scratch_shapes=[
            pltpu.VMEM((2, PLACES, rows, owned_wide), bf16),
            pltpu.VMEM((PLACES, 4, rows, block), bf16),
            pltpu.VMEM((PLACES, 4, rows, block), bf16),
            pltpu.VMEM((PLACES, RIDERS, owned_wide), bf16),
        ],
        compiler_params=pltpu.CompilerParams(vmem_limit_bytes=14 * 2**20),
        cost_estimate=pl.CostEstimate(
            flops=35 * 10**9, bytes_accessed=38 * 10**6, transcendentals=0
        ),
        name="chain",
    )(order, *fields, *choices, factors, matrices)


    results, gram, inverse = pl.pallas_call(
        dots_kernel,
        out_shape=(
            jax.ShapeDtypeStruct((4, loads, owned_wide), f32),
            jax.ShapeDtypeStruct((devices, 8, LANES), f32),
            jax.ShapeDtypeStruct((devices, LANES), f32),
        ),
        in_specs=[smem] + [vmem] * 4,
        out_specs=(vmem,) * 3,
        scratch_shapes=[pltpu.VMEM((devices, LANES), f32), pltpu.VMEM((LANES, LANES), f32)],
        compiler_params=pltpu.CompilerParams(vmem_limit_bytes=8 * 2**20),
        name="dots",
    )(order, own, packed, shared, wide)

    gathered = lax.all_to_all(gram, axes, split_axis=0, concat_axis=0, tiled=True)
    iterate, residual = pl.pallas_call(
        finish_kernel,
        out_shape=(jax.ShapeDtypeStruct((owned_count, 1, loads), f32),) * 2,
        in_specs=[smem] + [vmem] * 6,
        out_specs=(anywhere, anywhere),
        scratch_shapes=[
            pltpu.VMEM((devices, LANES), f32),
            pltpu.VMEM((LANES, LANES), f32),
            pltpu.VMEM((owned_wide, loads), f32),
            pltpu.VMEM((owned_wide, loads), f32),
            pltpu.SemaphoreType.DMA((2, owned_wide // LANES)),
        ],
        compiler_params=pltpu.CompilerParams(vmem_limit_bytes=8 * 2**20),
        name="finish",
    )(order, gathered, inverse, results, own, wide, padded)
    return (iterate.reshape(forces.shape), residual.reshape(forces.shape))


def spread_owned(values, slot_rows):
    padded = jnp.concatenate([values, jnp.zeros((1, values.shape[1]), values.dtype)], axis=0)
    return jnp.take(padded, slot_rows, axis=0)


def element_block(copies, matrix, factors, divide):
    columns = copies.shape[-1]
    blocks = copies.reshape(factors.shape[0], matrix.shape[0], columns)
    product = jnp.einsum("ab,ebr->ear", matrix, blocks, preferred_element_type=jnp.float32)
    if divide:
        scaled = product / factors[:, None, None]
    else:
        scaled = product * factors[:, None, None]
    return scaled.astype(jnp.bfloat16).reshape(-1, columns)


def exchange_body(
    forces,
    stiffness,
    local_solve,
    moduli,
    coarse_basis,
    coarse_inverse,
    send_index,
    owner_slot,
    home_slot,
):
    loaded = forces[0, 0]
    owned_count = loaded.shape[0]
    send_rows = send_index[0, 0]
    slot_rows = owner_slot[0, 0]
    home_rows = home_slot[0, 0]
    elastic = moduli[0, 0]
    basis_values = coarse_basis[0, 0]
    groups, capacity = send_rows.shape
    block_size = stiffness.shape[0]
    inner_count = elastic.shape[0] // 2
    border_start = inner_count * block_size
    local_count = home_rows.shape[0]
    inner_elastic = elastic[:inner_count]
    outer_elastic = elastic[inner_count:]
    sent_position = (
        jnp.zeros((local_count + 1,), jnp.int32)
        .at[send_rows.reshape(-1)]
        .set(jnp.arange(groups * capacity, dtype=jnp.int32))[:local_count]
    )
    position = jnp.where(home_rows < owned_count, groups * capacity + home_rows, sent_position)
    inner_home = home_rows[:border_start]
    outer_rows = position[border_start:]
    gather_rows = jnp.concatenate([slot_rows.reshape(-1), home_rows], axis=0)
    device = lax.axis_index(("sub", "grp"))
    full_inverse = lax.all_gather(coarse_inverse, ("sub", "grp"), axis=0, tiled=True)

    def joined(received, own_values):
        columns = received.shape[2]
        return jnp.concatenate([received.reshape(-1, columns), own_values], axis=0)

    def return_terms(inner_terms, outer_copies, matrix, divide):
        outer_terms = element_block(outer_copies, matrix, outer_elastic, divide)
        element_terms = jnp.concatenate([inner_terms, outer_terms], axis=0)
        columns = element_terms.shape[1]
        padded = jnp.concatenate(
            [element_terms, jnp.zeros((1, columns), element_terms.dtype)], axis=0
        )
        outgoing = jnp.take(padded, send_rows, axis=0)
        returned = lax.all_to_all(outgoing, "grp", split_axis=0, concat_axis=0, tiled=True)
        contributions = jnp.concatenate(
            [returned.reshape(-1, columns), element_terms], axis=0
        ).astype(jnp.float32)
        summed = (
            jnp.zeros((owned_count + 1, columns), jnp.float32).at[gather_rows].add(contributions)
        )
        return summed[:owned_count]

    def residual_solve(residual):
        own_copy = residual.astype(jnp.bfloat16)
        inner_terms = element_block(
            jnp.take(own_copy, inner_home, axis=0), local_solve, inner_elastic, True
        )
        received = lax.all_to_all(
            spread_owned(own_copy, slot_rows), "grp", split_axis=0, concat_axis=0, tiled=True
        )
        outer_copies = jnp.take(joined(received, own_copy), outer_rows, axis=0)
        return return_terms(inner_terms, outer_copies, local_solve, True)

    def coarse_step(residual, local_part):
        own_term = jnp.dot(basis_values[None, :], residual, precision=lax.Precision.HIGHEST)
        spread = jnp.zeros((full_inverse.shape[0], own_term.shape[1]), jnp.float32)
        spread = lax.dynamic_update_slice(spread, own_term, (device, jnp.int32(0)))
        totals, partial_value = lax.psum(
            (spread, jnp.sum(residual * local_part, axis=0)), ("sub", "grp")
        )
        answer = jnp.dot(full_inverse, totals, precision=lax.Precision.HIGHEST)
        own_answer = lax.dynamic_slice_in_dim(answer, device, 1, 0)
        search = local_part + basis_values[:, None] * own_answer
        weighted = partial_value + jnp.sum(totals * answer, axis=0)
        return (search, weighted)

    solution = jnp.zeros_like(loaded)
    residual = loaded
    local_part = residual_solve(residual)
    search, weighted = coarse_step(residual, local_part)
    direction = search
    for iteration in range(ITERS):
        apply_own_copy = direction.astype(jnp.bfloat16)
        apply_inner_terms = element_block(
            jnp.take(apply_own_copy, inner_home, axis=0), stiffness, inner_elastic, False
        )
        apply_received = lax.all_to_all(
            spread_owned(apply_own_copy, slot_rows), "grp", split_axis=0, concat_axis=0, tiled=True
        )
        apply_outer_copies = jnp.take(joined(apply_received, apply_own_copy), outer_rows, axis=0)
        image_field = return_terms(apply_inner_terms, apply_outer_copies, stiffness, False)
        final_turn = iteration + 1 == ITERS
        curvature = lax.psum(jnp.sum(direction * image_field, axis=0), ("sub", "grp"))
        step_size = weighted / curvature
        solution = solution + step_size[None, :] * direction
        residual = residual - step_size[None, :] * image_field
        if not final_turn:
            local_part = residual_solve(residual)
            search, update = coarse_step(residual, local_part)
            direction = search + (update / weighted)[None, :] * direction
            weighted = update
    return (solution[None, None], residual[None, None])


def solution(mesh):
    if mesh.shape["grp"] == PLACES:
        body = functools.partial(slab_body, dict(mesh.shape))
    else:
        body = exchange_body
    return jax.shard_map(
        body,
        mesh=mesh,
        in_specs=(
            P("sub", "grp", None, None),
            P(),
            P(),
            P("sub", "grp", None),
            P("sub", "grp", None),
            P(("sub", "grp"), None),
            P("sub", "grp", None, None),
            P("sub", "grp", None, None),
            P("sub", "grp", None),
        ),
        out_specs=(P("sub", "grp", None, None), P("sub", "grp", None, None)),
        check_vma=False,
    )
```

```python
import functools

import jax
import jax.numpy as jnp
from jax import lax
from jax.experimental import pallas as pl
from jax.experimental.pallas import tpu as pltpu
from jax.sharding import PartitionSpec as P

ITERS = 2
LANES = 128
RIDERS = 16
PLACES = 4


def round_up(value, unit):
    return -(-value // unit) * unit


def place_distances(order_ref):
    return [0] + [order_ref[place - 1] for place in range(1, PLACES)]


def turn(ref, rows, width):
    return ref[rows : rows + LANES, :width].T


def pack_kernel(
    forces_hbm,
    basis_hbm,
    inverse_hbm,
    send_hbm,
    owner_hbm,
    home_hbm,
    moduli_hbm,
    stiffness_hbm,
    solve_hbm,
    packed_ref,
    table_ref,
    shared_ref,
    padded,
    wide_ref,
    order_ref,
    matrices_ref,
    basis_ref,
    inverse_ref,
    send_ref,
    owner_ref,
    home_ref,
    moduli_ref,
    stiffness_ref,
    solve_ref,
    square,
    arrived,
):
    f32, bf16 = jnp.float32, jnp.bfloat16
    owned, _, loads = forces_hbm.shape
    wide = padded.shape[0]
    half = table_ref.shape[1]
    members, capacity = send_ref.shape
    local = home_ref.shape[1]
    slab, member = lax.axis_index("sub"), lax.axis_index("grp")
    copies = [
        pltpu.make_async_copy(source, target, arrived.at[at])
        for at, (source, target) in enumerate(
            (
                (forces_hbm.at[:, 0, :], padded.at[:owned, :]),
                (basis_hbm, basis_ref),
                (inverse_hbm, inverse_ref),
                (send_hbm, send_ref),
                (owner_hbm, owner_ref),
                (home_hbm, home_ref),
                (moduli_hbm, moduli_ref),
                (stiffness_hbm, stiffness_ref),
                (solve_hbm, solve_ref),
            )
        )
    ]
    for copy in copies:
        copy.start()
    padded[owned:, :] = jnp.zeros((wide - owned, loads), f32)
    wide_ref[...] = jnp.zeros_like(wide_ref)
    table_ref[...] = jnp.full(table_ref.shape, -1.0, f32)
    matrices_ref[...] = jnp.zeros_like(matrices_ref)
    for copy in copies:
        copy.wait()
    size = stiffness_ref.shape[0]
    matrices_ref[0, :size, :size] = stiffness_ref[...]
    matrices_ref[1, :size, :size] = solve_ref[...]

    apart = lax.broadcasted_iota(jnp.int32, (members, LANES), 0) ^ member
    unused = (send_ref[:, :LANES] >= local) & (apart > 0)
    unused = unused & (lax.broadcasted_iota(jnp.int32, (members, LANES), 1) == 0)
    opposite = jnp.sum(jnp.where(unused, apart.astype(f32), 0.0)).astype(jnp.int32)
    opposite = jnp.minimum(jnp.maximum(opposite, 1), PLACES - 1)
    near = jnp.where(opposite == 1, 2, 1)
    order = (near, opposite, 6 - near - opposite, member, slab, slab, slab, slab)
    for at, value in enumerate(order):
        order_ref[at] = value

    wide_ref[0:1, :owned] = basis_ref[...]
    basis = wide_ref[0:1, :]
    term = jnp.zeros((loads, 1), f32)
    for start in range(0, wide, LANES):
        turned = padded[start : start + LANES, :].T
        packed_ref[:, start : start + LANES] = turned.astype(bf16)
        term = term + jnp.sum(
            turned * basis[:, start : start + LANES], axis=1, keepdims=True
        )

    table_ref[0:1, :] = home_ref[:, :half].astype(f32)
    table_ref[1:2, : local - half] = home_ref[:, half:].astype(f32)
    table_ref[2 : 2 + members, :capacity] = send_ref[...].astype(f32)
    table_ref[2 : 2 + members, half // 2 : half // 2 + capacity] = owner_ref[...].astype(f32)
    table_ref[6:7, :] = basis
    square[...] = jnp.broadcast_to(term, square.shape)
    own_term = square[...].T[0:1, :]
    square[0:1, :] = own_term
    square[1:2, :] = jnp.zeros((1, LANES), f32)
    square[1:2, : inverse_ref.shape[1]] = inverse_ref[...]
    shared_ref[...] = jnp.broadcast_to(square[0:2, :][None], shared_ref.shape)
    table_ref[7:8, : moduli_ref.shape[1]] = moduli_ref[...]


def build_kernel(
    size,
    owned_count,
    local_count,
    order_ref,
    t0_ref,
    t1_ref,
    t2_ref,
    t3_ref,
    pick0,
    pick1,
    pick2,
    pick3,
    put0,
    put1,
    put2,
    put3,
    factors,
    riders,
    tables,
    slots,
    homes,
    sources,
    sources_t,
):
    picks, puts = (pick0, pick1, pick2, pick3), (put0, put1, put2, put3)
    owned, half = pick0.shape[1], pick0.shape[2]
    block = half // 2
    slot_count = slots.shape[1]
    f32, bf16 = jnp.float32, jnp.bfloat16
    distance = place_distances(order_ref)
    member = order_ref[3]
    elements = 4
    for at, table_ref in enumerate((t0_ref, t1_ref, t2_ref, t3_ref)):
        tables[at] = table_ref[...]
    sources[...] = jnp.full(sources.shape, -1.0, f32)
    slots[...] = jnp.full(slots.shape, -1.0, f32)
    homes[...] = jnp.zeros_like(homes)
    lane_block = lax.broadcasted_iota(jnp.int32, (8, block), 1)
    rider_ids = lax.broadcasted_iota(jnp.int32, (RIDERS, owned), 0)
    for place in range(PLACES):
        riders[place] = jnp.where(
            rider_ids == place, tables[distance[place], 6:7, :], 0.0
        ).astype(bf16)
        homes[place : place + 1, :half] = tables[distance[place], 0:1, :]
        homes[place : place + 1, half:] = tables[distance[place], 1:2, :]
        for e in range(elements):
            modulus = jnp.broadcast_to(tables[distance[place], 7:8, e : e + 1], (1, block))
            factors[0, place, e : e + 1, :] = modulus
            factors[1, place, e : e + 1, :] = 1.0 / modulus

    all_homes = homes[...]
    for e in range(elements):
        shift = (all_homes.shape[1] - e * size) % all_homes.shape[1]
        moved = all_homes if e == 0 else pltpu.roll(all_homes, shift, 1)
        rows = moved[:, :block]
        rows = jnp.where((lane_block < size) & (rows < float(owned_count)), rows, -1.0)
        part, column = e // 2, (e % 2) * block
        sources[part * PLACES : (part + 1) * PLACES, column : column + block] = rows[:PLACES]

    pairs = [(a, (a + step) % PLACES) for step in (1, PLACES - 1) for a in range(PLACES)]
    for pair, (reader, owner) in enumerate(pairs):
        to_owner = pl.ds(2 + (member ^ distance[owner]), 1)
        to_reader = pl.ds(2 + (member ^ distance[reader]), 1)
        sent = tables[distance[reader], to_owner, :slot_count]
        sent = jnp.where(sent < float(local_count), sent, -1.0)
        first = float(2 * size)
        moved = sent - first + jnp.where(sent >= first + size, float(block - size), 0.0)
        slots[2 * pair : 2 * pair + 1, :] = jnp.where(sent < 0.0, -1.0, moved)
        slots[2 * pair + 1 : 2 * pair + 2, :] = tables[distance[owner], to_reader, slot_count:]
    slots_t = slots[...].T
    half_ids = lax.broadcasted_iota(jnp.int32, (LANES, half), 1).astype(f32)
    for pair in range(len(pairs)):
        found = jnp.zeros((1, half), f32)
        for start in range(0, slot_count, LANES):
            column = slots_t[start : start + LANES, 2 * pair : 2 * pair + 1]
            target = slots_t[start : start + LANES, 2 * pair + 1 : 2 * pair + 2] + 1.0
            found = found + jnp.sum(
                jnp.where(half_ids == column, target, 0.0), axis=0, keepdims=True
            )
        sources[2 * PLACES + pair : 2 * PLACES + pair + 1, :] = found - 1.0
    sources_t[...] = sources[...].T

    chunk = 256
    deep_ids = lax.broadcasted_iota(jnp.int32, (chunk, LANES), 0).astype(f32).astype(bf16)
    lane_ids = lax.broadcasted_iota(jnp.int32, (chunk, chunk), 1).astype(f32).astype(bf16)
    column_ids = lax.broadcasted_iota(jnp.int32, (chunk, LANES), 1)
    one, zero = jnp.ones((), bf16), jnp.zeros((), bf16)

    for kind, (pick, put) in enumerate(zip(picks, puts)):

        def build(place, carry):
            n = kind * PLACES + place
            source = sources[pl.ds(n, 1), :]
            for start in range(0, owned, chunk):
                moved = (source - float(start)).astype(bf16)
                for at in range(0, half, LANES):
                    wanted = jnp.broadcast_to(moved[:, at : at + LANES], (chunk, LANES))
                    pick[place, start : start + chunk, at : at + LANES] = jnp.where(
                        deep_ids == wanted, one, zero
                    )
            for start in range(0, half, chunk):
                column = jnp.sum(
                    jnp.where(column_ids == n, sources_t[start : start + chunk, :], 0.0),
                    axis=1,
                    keepdims=True,
                )
                for at in range(0, owned, chunk):
                    wanted = jnp.broadcast_to(column - float(at), (chunk, LANES)).astype(bf16)
                    wanted = jnp.concatenate([wanted] * (chunk // LANES), axis=1)
                    put[place, start : start + chunk, at : at + chunk] = jnp.where(
                        lane_ids == wanted, one, zero
                    )
            return carry

        lax.fori_loop(0, PLACES, build, 0)


def chain_kernel(
    order_ref,
    x0_ref,
    x1_ref,
    x2_ref,
    x3_ref,
    pick0,
    pick1,
    pick2,
    pick3,
    put0,
    put1,
    put2,
    put3,
    factors,
    riders,
    matrices_ref,
    own,
    values,
    terms,
    copies,
):
    owned, half = pick0.shape[1], pick0.shape[2]
    block = matrices_ref.shape[1]
    rows = own.shape[1]
    loads = rows - RIDERS
    f32, bf16 = jnp.float32, jnp.bfloat16
    distance = place_distances(order_ref)
    for at, x_ref in enumerate((x0_ref, x1_ref, x2_ref, x3_ref)):
        values[1, at, :loads, :] = x_ref[...]
    for place in range(PLACES):
        values[0, place, :loads, :] = values[1, distance[place], :loads, :]
        values[0, place, loads:, :] = jnp.zeros((RIDERS, owned), bf16)

    def multiply(left, right):
        return jnp.dot(left, right, preferred_element_type=f32)

    def beside(refs):
        return jnp.concatenate(refs, axis=1)

    def above(refs):
        return jnp.concatenate(refs, axis=0)

    def split(place, part, copied):
        copied = copied.astype(bf16)
        copies[place, 2 * part] = copied[:, :block]
        copies[place, 2 * part + 1] = copied[:, block:]

    def inner(source, place):
        split(place, 0, multiply(values[source, place], pick0[place]))

    def outer(source, place):
        ahead, behind = (place + 1) % PLACES, (place - 1) % PLACES
        fields = beside([values[source, at] for at in (place, ahead, behind)])
        split(place, 1, multiply(fields, above([pick1[place], pick2[place], pick3[place]])))

    def scaled(which, at, count):
        product = multiply(copies[at].reshape(count * 4 * rows, block), matrices_ref[which])
        scale = factors[which, at].reshape(count, 4, 1, block)
        terms[at] = (product.reshape(count, 4, rows, block) * scale).astype(bf16)

    def collect(place):
        ahead, behind = (place + 1) % PLACES, (place - 1) % PLACES
        ends = beside(
            [terms[place, e] for e in range(4)]
            + [terms[behind, 2], terms[behind, 3], terms[ahead, 2], terms[ahead, 3]]
        )
        return multiply(ends, above([put0[place], put1[place], put2[behind], put3[ahead]]))

    def stage(at, carry):
        which = lax.rem(at + 1, 2)
        source, target = lax.rem(at, 2), lax.rem(at + 1, 2)
        for place in range(PLACES):
            inner(source, place)
            outer(source, place)
        scaled(which, slice(0, PLACES), PLACES)
        for place in range(PLACES):
            summed = collect(place)
            values[target, place] = summed.astype(bf16)
            if place == 0:
                own[at] = summed

        @pl.when(at == 0)
        def _():
            for place in range(PLACES):
                values[1, place, loads:, :] = riders[place]

        return carry

    lax.fori_loop(0, 3, stage, 0)
    inner(1, 0)
    outer(1, 0)
    outer(1, 1)
    outer(1, 3)
    scaled(0, slice(0, 2), 2)
    scaled(0, slice(3, 4), 1)
    own[3] = collect(0)


def dots_kernel(
    order_ref,
    own,
    x0_ref,
    shared_ref,
    wide_ref,
    fields_ref,
    images_ref,
    gram_ref,
    inverse,
    coarse_ref,
    square,
):
    f32 = jnp.float32
    loads = fields_ref.shape[1]
    distance = place_distances(order_ref)
    devices = inverse.shape[0]
    member = order_ref[3]
    first = order_ref[4] * PLACES
    coarse_ref[...] = shared_ref[:, 0, :]
    inverse[...] = shared_ref[:, 1, :]
    square[...] = jnp.zeros_like(square)
    for place in range(PLACES):
        square[place : place + 1, :] = inverse[pl.ds(first + (member ^ distance[place]), 1), :]
    answer = jnp.dot(
        square[0:8, :devices],
        coarse_ref[...],
        precision=lax.Precision.HIGHEST,
        preferred_element_type=f32,
    )
    square[...] = jnp.zeros_like(square)
    square[0:8, :] = answer
    answer_t = square[...].T
    basis = wide_ref[0:1, :]
    start_field = own[0, :loads, :] + answer_t[:, 0:1] * basis
    start_image = own[1, :loads, :]
    next_field = own[2, :loads, :]
    next_image = own[3, :loads, :]
    for place in range(PLACES):
        column = answer_t[:, place : place + 1]
        row = loads + place
        start_image = start_image + column * own[1, row : row + 1, :]
        next_field = next_field + column * own[2, row : row + 1, :]
        next_image = next_image + column * own[3, row : row + 1, :]
    fields_ref[0] = start_field
    fields_ref[1] = next_field
    fields_ref[2] = start_image
    fields_ref[3] = next_image
    images_ref[...] = own[1, loads : loads + 8, :]
    residual = x0_ref[...].astype(f32)
    lanes = lax.broadcasted_iota(jnp.int32, square.shape, 1)
    collected = jnp.zeros(square.shape, f32)
    for at, product in enumerate(
        (
            residual * start_field,
            start_field * start_image,
            start_image * next_field,
            next_field * next_image,
            basis * start_image,
            basis * next_image,
        )
    ):
        total = jnp.sum(product, axis=1, keepdims=True)
        collected = jnp.where(lanes == at, total, collected)
    gram = collected.T[0:8, :]
    row_at = lax.broadcasted_iota(jnp.int32, gram.shape, 0)
    lane_at = lax.broadcasted_iota(jnp.int32, gram.shape, 1)
    for place in range(PLACES):
        entry = jnp.sum(
            basis * own[1, loads + place : loads + place + 1, :], axis=1, keepdims=True
        )
        here = (row_at == 6) & (lane_at == first + (member ^ distance[place]))
        gram = jnp.where(here, entry, gram)
    gram_ref[...] = jnp.broadcast_to(gram[None], gram_ref.shape)


def finish_kernel(
    order_ref,
    gram_ref,
    inverse,
    fields_ref,
    images_ref,
    wide_ref,
    padded,
    solution_hbm,
    residual_hbm,
    answer,
    square,
    iterates,
    residuals,
    sent,
):
    f32 = jnp.float32
    count = inverse.shape[0]
    owned = solution_hbm.shape[0]
    first = order_ref[4] * PLACES
    member = order_ref[3]
    distance = place_distances(order_ref)
    precise = functools.partial(
        jnp.dot, precision=lax.Precision.HIGHEST, preferred_element_type=f32
    )
    coarse = gram_ref[:, 4, :]
    answer[...] = precise(inverse[:, :count], coarse)
    answers = answer[...]
    mixed = precise(gram_ref[:, 6, :count], answers)
    sums = jnp.sum(gram_ref[...], axis=0)
    weighted, curvature = sums[0:1, :], sums[1:2, :]
    cross = sums[2:3, :] + jnp.sum(coarse * answers, axis=0, keepdims=True)
    last = sums[3:4, :] + jnp.sum(
        answers * (2.0 * gram_ref[:, 5, :] + mixed), axis=0, keepdims=True
    )
    step = weighted / curvature
    update = step * step * cross - weighted
    grown = 1.0 + update / weighted
    curvature = grown * grown * curvature - 2.0 * step * grown * cross + step * step * last
    second = update / curvature
    whole = step + second * grown
    back = step * second
    square[...] = jnp.zeros_like(square)
    square[0:1, :] = whole
    square[1:2, :] = back
    for place in range(PLACES):
        at = first + (member ^ distance[place])
        square[2 + place : 3 + place, :] = back * answer[pl.ds(at, 1), :]
    columns = square[...].T
    whole, back = columns[:, 0:1], columns[:, 1:2]
    copies = []
    for start in range(0, wide_ref.shape[1], LANES):
        part = slice(start, start + LANES)
        size = min(LANES, owned - start)
        iterate = (
            whole * fields_ref[0, :, part]
            - back * fields_ref[1, :, part]
            - columns[:, 2:3] * wide_ref[0:1, part]
        )
        change = back * fields_ref[3, :, part] - whole * fields_ref[2, :, part]
        for place in range(PLACES):
            image = images_ref[place : place + 1, part]
            change = change + columns[:, 2 + place : 3 + place] * image
        iterates[start : start + LANES, :] = iterate.T
        residuals[start : start + LANES, :] = padded[start : start + LANES, :] + change.T
        rows = slice(start, start + size)
        for at, (source, target) in enumerate(
            ((iterates, solution_hbm), (residuals, residual_hbm))
        ):
            copy = pltpu.make_async_copy(
                source.at[rows, :], target.at[rows, 0, :], sent.at[at, start // LANES]
            )
            copy.start()
            copies.append(copy)
    for copy in copies:
        copy.wait()


def slab_body(
    mesh_shape,
    forces,
    stiffness,
    local_solve,
    moduli,
    coarse_basis,
    coarse_inverse,
    send_index,
    owner_slot,
    home_slot,
):
    f32, bf16, i32 = jnp.float32, jnp.bfloat16, jnp.int32
    axes = ("sub", "grp")
    owned_count, loads = forces.shape[2:]
    size = stiffness.shape[0]
    local_count = home_slot.shape[2]
    owned_wide = round_up(owned_count, 256)
    block = round_up(size, LANES)
    half = 2 * block
    devices = mesh_shape["sub"] * mesh_shape["grp"]
    rows = loads + RIDERS
    fits = half == owned_wide and loads == LANES and moduli.shape[2] == 4
    fits = fits and send_index.shape[3] <= half // 2 and devices <= LANES
    if not fits:
        return exchange_body(
            forces,
            stiffness,
            local_solve,
            moduli,
            coarse_basis,
            coarse_inverse,
            send_index,
            owner_slot,
            home_slot,
        )
    smem = pl.BlockSpec(memory_space=pltpu.SMEM)
    vmem = pl.BlockSpec(memory_space=pltpu.VMEM)

    anywhere = pl.BlockSpec(memory_space=pltpu.HBM)
    slabs = mesh_shape["sub"]

    packed, table, shared, padded, wide, order, matrices = pl.pallas_call(
        pack_kernel,
        out_shape=(
            jax.ShapeDtypeStruct((loads, owned_wide), bf16),
            jax.ShapeDtypeStruct((8, half), f32),
            jax.ShapeDtypeStruct((devices, 2, LANES), f32),
            jax.ShapeDtypeStruct((owned_wide, loads), f32),
            jax.ShapeDtypeStruct((8, owned_wide), f32),
            jax.ShapeDtypeStruct((8,), i32),
            jax.ShapeDtypeStruct((2, block, block), bf16),
        ),
        in_specs=[anywhere] * 9,
        out_specs=(vmem,) * 5 + (smem, vmem),
        scratch_shapes=[
            pltpu.VMEM((1, owned_count), f32),
            pltpu.VMEM((1, devices), f32),
            pltpu.VMEM(send_index.shape[2:], i32),
            pltpu.VMEM(owner_slot.shape[2:], i32),
            pltpu.VMEM((1, local_count), i32),
            pltpu.VMEM((1, moduli.shape[2]), f32),
            pltpu.VMEM((size, size), bf16),
            pltpu.VMEM((size, size), bf16),
            pltpu.VMEM((LANES, LANES), f32),
            pltpu.SemaphoreType.DMA((9,)),
        ],
        compiler_params=pltpu.CompilerParams(vmem_limit_bytes=62 * 2**20),
        name="pack",
    )(
        forces.reshape(owned_count, 1, loads),
        coarse_basis[0],
        coarse_inverse,
        send_index[0, 0],
        owner_slot[0, 0],
        home_slot[0],
        moduli[0],
        stiffness,
        local_solve,
    )

    def swapped(array, distance):
        return lax.ppermute(array, "grp", [(i, i ^ distance) for i in range(PLACES)])

    near_table = swapped(table, 1)
    late, near_table = lax.optimization_barrier((packed, near_table))
    tables = [table, near_table, swapped(table, 2), swapped(table, 3)]
    fields = [packed, swapped(late, 1), swapped(packed, 2), swapped(packed, 3)]
    shared = lax.all_to_all(shared, axes, split_axis=0, concat_axis=0, tiled=True)

    *choices, factors, riders = pl.pallas_call(
        functools.partial(build_kernel, size, owned_count, local_count),
        out_shape=(
            *[jax.ShapeDtypeStruct((PLACES, owned_wide, half), bf16)] * 4,
            *[jax.ShapeDtypeStruct((PLACES, half, owned_wide), bf16)] * 4,
            jax.ShapeDtypeStruct((2, PLACES, 4, block), f32),
            jax.ShapeDtypeStruct((PLACES, RIDERS, owned_wide), bf16),
        ),
        in_specs=[smem] + [vmem] * 4,
        out_specs=(vmem,) * 10,
        scratch_shapes=[
            pltpu.VMEM((PLACES, 8, half), f32),
            pltpu.VMEM((LANES, half // 2), f32),
            pltpu.VMEM((8, 2 * half), f32),
            pltpu.VMEM((LANES, half), f32),
            pltpu.VMEM((half, LANES), f32),
        ],
        compiler_params=pltpu.CompilerParams(vmem_limit_bytes=4 * 2**20),
        cost_estimate=pl.CostEstimate(
            flops=8 * 10**9, bytes_accessed=38 * 10**6, transcendentals=0
        ),
        name="build",
    )(order, *tables)

    own = pl.pallas_call(
        chain_kernel,
        out_shape=jax.ShapeDtypeStruct((4, rows, owned_wide), f32),
        in_specs=[smem] + [vmem] * 15,
        out_specs=vmem,
        scratch_shapes=[
            pltpu.VMEM((2, PLACES, rows, owned_wide), bf16),
            pltpu.VMEM((PLACES, 4, rows, block), bf16),
            pltpu.VMEM((PLACES, 4, rows, block), bf16),
        ],
        compiler_params=pltpu.CompilerParams(vmem_limit_bytes=9 * 2**20),
        cost_estimate=pl.CostEstimate(
            flops=35 * 10**9, bytes_accessed=38 * 10**6, transcendentals=0
        ),
        name="chain",
    )(order, *fields, *choices, factors, riders, matrices)

    results, images, gram, inverse = pl.pallas_call(
        dots_kernel,
        out_shape=(
            jax.ShapeDtypeStruct((4, loads, owned_wide), f32),
            jax.ShapeDtypeStruct((8, owned_wide), f32),
            jax.ShapeDtypeStruct((devices, 8, LANES), f32),
            jax.ShapeDtypeStruct((devices, LANES), f32),
        ),
        in_specs=[smem] + [vmem] * 4,
        out_specs=(vmem,) * 4,
        scratch_shapes=[pltpu.VMEM((devices, LANES), f32), pltpu.VMEM((LANES, LANES), f32)],
        compiler_params=pltpu.CompilerParams(vmem_limit_bytes=4 * 2**20),
        name="dots",
    )(order, own, packed, shared, wide)

    gathered = lax.all_to_all(gram, axes, split_axis=0, concat_axis=0, tiled=True)
    iterate, residual = pl.pallas_call(
        finish_kernel,
        out_shape=(jax.ShapeDtypeStruct((owned_count, 1, loads), f32),) * 2,
        in_specs=[smem] + [vmem] * 6,
        out_specs=(anywhere, anywhere),
        scratch_shapes=[
            pltpu.VMEM((devices, LANES), f32),
            pltpu.VMEM((LANES, LANES), f32),
            pltpu.VMEM((owned_wide, loads), f32),
            pltpu.VMEM((owned_wide, loads), f32),
            pltpu.SemaphoreType.DMA((2, owned_wide // LANES)),
        ],
        compiler_params=pltpu.CompilerParams(vmem_limit_bytes=4 * 2**20),
        name="finish",
    )(order, gathered, inverse, results, images, wide, padded)
    return (iterate.reshape(forces.shape), residual.reshape(forces.shape))


def spread_owned(values, slot_rows):
    padded = jnp.concatenate([values, jnp.zeros((1, values.shape[1]), values.dtype)], axis=0)
    return jnp.take(padded, slot_rows, axis=0)


def element_block(copies, matrix, factors, divide):
    columns = copies.shape[-1]
    blocks = copies.reshape(factors.shape[0], matrix.shape[0], columns)
    product = jnp.einsum("ab,ebr->ear", matrix, blocks, preferred_element_type=jnp.float32)
    if divide:
        scaled = product / factors[:, None, None]
    else:
        scaled = product * factors[:, None, None]
    return scaled.astype(jnp.bfloat16).reshape(-1, columns)


def exchange_body(
    forces,
    stiffness,
    local_solve,
    moduli,
    coarse_basis,
    coarse_inverse,
    send_index,
    owner_slot,
    home_slot,
):
    loaded = forces[0, 0]
    owned_count = loaded.shape[0]
    send_rows = send_index[0, 0]
    slot_rows = owner_slot[0, 0]
    home_rows = home_slot[0, 0]
    elastic = moduli[0, 0]
    basis_values = coarse_basis[0, 0]
    groups, capacity = send_rows.shape
    block_size = stiffness.shape[0]
    inner_count = elastic.shape[0] // 2
    border_start = inner_count * block_size
    local_count = home_rows.shape[0]
    inner_elastic = elastic[:inner_count]
    outer_elastic = elastic[inner_count:]
    sent_position = (
        jnp.zeros((local_count + 1,), jnp.int32)
        .at[send_rows.reshape(-1)]
        .set(jnp.arange(groups * capacity, dtype=jnp.int32))[:local_count]
    )
    position = jnp.where(home_rows < owned_count, groups * capacity + home_rows, sent_position)
    inner_home = home_rows[:border_start]
    outer_rows = position[border_start:]
    gather_rows = jnp.concatenate([slot_rows.reshape(-1), home_rows], axis=0)
    device = lax.axis_index(("sub", "grp"))
    full_inverse = lax.all_gather(coarse_inverse, ("sub", "grp"), axis=0, tiled=True)

    def joined(received, own_values):
        columns = received.shape[2]
        return jnp.concatenate([received.reshape(-1, columns), own_values], axis=0)

    def return_terms(inner_terms, outer_copies, matrix, divide):
        outer_terms = element_block(outer_copies, matrix, outer_elastic, divide)
        element_terms = jnp.concatenate([inner_terms, outer_terms], axis=0)
        columns = element_terms.shape[1]
        padded = jnp.concatenate(
            [element_terms, jnp.zeros((1, columns), element_terms.dtype)], axis=0
        )
        outgoing = jnp.take(padded, send_rows, axis=0)
        returned = lax.all_to_all(outgoing, "grp", split_axis=0, concat_axis=0, tiled=True)
        contributions = jnp.concatenate(
            [returned.reshape(-1, columns), element_terms], axis=0
        ).astype(jnp.float32)
        summed = (
            jnp.zeros((owned_count + 1, columns), jnp.float32).at[gather_rows].add(contributions)
        )
        return summed[:owned_count]

    def residual_solve(residual):
        own_copy = residual.astype(jnp.bfloat16)
        inner_terms = element_block(
            jnp.take(own_copy, inner_home, axis=0), local_solve, inner_elastic, True
        )
        received = lax.all_to_all(
            spread_owned(own_copy, slot_rows), "grp", split_axis=0, concat_axis=0, tiled=True
        )
        outer_copies = jnp.take(joined(received, own_copy), outer_rows, axis=0)
        return return_terms(inner_terms, outer_copies, local_solve, True)

    def coarse_step(residual, local_part):
        own_term = jnp.dot(basis_values[None, :], residual, precision=lax.Precision.HIGHEST)
        spread = jnp.zeros((full_inverse.shape[0], own_term.shape[1]), jnp.float32)
        spread = lax.dynamic_update_slice(spread, own_term, (device, jnp.int32(0)))
        totals, partial_value = lax.psum(
            (spread, jnp.sum(residual * local_part, axis=0)), ("sub", "grp")
        )
        answer = jnp.dot(full_inverse, totals, precision=lax.Precision.HIGHEST)
        own_answer = lax.dynamic_slice_in_dim(answer, device, 1, 0)
        search = local_part + basis_values[:, None] * own_answer
        weighted = partial_value + jnp.sum(totals * answer, axis=0)
        return (search, weighted)

    solution = jnp.zeros_like(loaded)
    residual = loaded
    local_part = residual_solve(residual)
    search, weighted = coarse_step(residual, local_part)
    direction = search
    for iteration in range(ITERS):
        apply_own_copy = direction.astype(jnp.bfloat16)
        apply_inner_terms = element_block(
            jnp.take(apply_own_copy, inner_home, axis=0), stiffness, inner_elastic, False
        )
        apply_received = lax.all_to_all(
            spread_owned(apply_own_copy, slot_rows), "grp", split_axis=0, concat_axis=0, tiled=True
        )
        apply_outer_copies = jnp.take(joined(apply_received, apply_own_copy), outer_rows, axis=0)
        image_field = return_terms(apply_inner_terms, apply_outer_copies, stiffness, False)
        final_turn = iteration + 1 == ITERS
        curvature = lax.psum(jnp.sum(direction * image_field, axis=0), ("sub", "grp"))
        step_size = weighted / curvature
        solution = solution + step_size[None, :] * direction
        residual = residual - step_size[None, :] * image_field
        if not final_turn:
            local_part = residual_solve(residual)
            search, update = coarse_step(residual, local_part)
            direction = search + (update / weighted)[None, :] * direction
            weighted = update
    return (solution[None, None], residual[None, None])


def solution(mesh):
    if mesh.shape["grp"] == PLACES:
        body = functools.partial(slab_body, dict(mesh.shape))
    else:
        body = exchange_body
    return jax.shard_map(
        body,
        mesh=mesh,
        in_specs=(
            P("sub", "grp", None, None),
            P(),
            P(),
            P("sub", "grp", None),
            P("sub", "grp", None),
            P(("sub", "grp"), None),
            P("sub", "grp", None, None),
            P("sub", "grp", None, None),
            P("sub", "grp", None),
        ),
        out_specs=(P("sub", "grp", None, None), P("sub", "grp", None, None)),
        check_vma=False,
    )
```

```python
import functools

import jax
import jax.numpy as jnp
from jax import lax
from jax.experimental import pallas as pl
from jax.experimental.pallas import tpu as pltpu
from jax.sharding import PartitionSpec as P

ITERS = 2
LANES = 128
RIDERS = 16
PLACES = 4


def round_up(value, unit):
    return -(-value // unit) * unit


def place_distances(order_ref):
    return [0] + [order_ref[place - 1] for place in range(1, PLACES)]


def turn(ref, rows, width):
    return ref[rows : rows + LANES, :width].T


def pack_kernel(
    forces_hbm,
    basis_hbm,
    inverse_hbm,
    send_hbm,
    owner_hbm,
    home_hbm,
    moduli_hbm,
    packed_ref,
    table_ref,
    shared_ref,
    padded,
    wide_ref,
    order_ref,
    basis_ref,
    inverse_ref,
    send_ref,
    owner_ref,
    home_ref,
    moduli_ref,
    square,
    arrived,
):
    f32, bf16 = jnp.float32, jnp.bfloat16
    owned, _, loads = forces_hbm.shape
    wide = padded.shape[0]
    half = table_ref.shape[1]
    members, capacity = send_ref.shape
    local = home_ref.shape[1]
    slab, member = lax.axis_index("sub"), lax.axis_index("grp")
    copies = [
        pltpu.make_async_copy(source, target, arrived.at[at])
        for at, (source, target) in enumerate(
            (
                (forces_hbm.at[:, 0, :], padded.at[:owned, :]),
                (basis_hbm, basis_ref),
                (inverse_hbm, inverse_ref),
                (send_hbm, send_ref),
                (owner_hbm, owner_ref),
                (home_hbm, home_ref),
                (moduli_hbm, moduli_ref),
            )
        )
    ]
    for copy in copies:
        copy.start()
    padded[owned:, :] = jnp.zeros((wide - owned, loads), f32)
    wide_ref[...] = jnp.zeros_like(wide_ref)
    table_ref[...] = jnp.full(table_ref.shape, -1.0, f32)
    for copy in copies:
        copy.wait()
    apart = lax.broadcasted_iota(jnp.int32, (members, LANES), 0) ^ member
    unused = (send_ref[:, :LANES] >= local) & (apart > 0)
    unused = unused & (lax.broadcasted_iota(jnp.int32, (members, LANES), 1) == 0)
    opposite = jnp.sum(jnp.where(unused, apart.astype(f32), 0.0)).astype(jnp.int32)
    opposite = jnp.minimum(jnp.maximum(opposite, 1), PLACES - 1)
    near = jnp.where(opposite == 1, 2, 1)
    order = (near, opposite, 6 - near - opposite, member, slab, slab, slab, slab)
    for at, value in enumerate(order):
        order_ref[at] = value

    wide_ref[0:1, :owned] = basis_ref[...]
    basis = wide_ref[0:1, :]
    term = jnp.zeros((loads, 1), f32)
    for start in range(0, wide, LANES):
        turned = padded[start : start + LANES, :].T
        packed_ref[:, start : start + LANES] = turned.astype(bf16)
        term = term + jnp.sum(
            turned * basis[:, start : start + LANES], axis=1, keepdims=True
        )

    table_ref[0:1, :] = home_ref[:, :half].astype(f32)
    table_ref[1:2, : local - half] = home_ref[:, half:].astype(f32)
    table_ref[2 : 2 + members, :capacity] = send_ref[...].astype(f32)
    table_ref[2 : 2 + members, half // 2 : half // 2 + capacity] = owner_ref[...].astype(f32)
    table_ref[6:7, :] = basis
    square[...] = jnp.broadcast_to(term, square.shape)
    own_term = square[...].T[0:1, :]
    square[0:1, :] = own_term
    square[1:2, :] = jnp.zeros((1, LANES), f32)
    square[1:2, : inverse_ref.shape[1]] = inverse_ref[...]
    shared_ref[...] = jnp.broadcast_to(square[0:2, :][None], shared_ref.shape)
    table_ref[7:8, : moduli_ref.shape[1]] = moduli_ref[...]


def build_kernel(
    size,
    owned_count,
    local_count,
    order_ref,
    t0_ref,
    t1_ref,
    t2_ref,
    t3_ref,
    pick0,
    pick1,
    pick2,
    pick3,
    put0,
    put1,
    put2,
    put3,
    factors,
    riders,
    tables,
    slots,
    homes,
    sources,
    sources_t,
):
    picks, puts = (pick0, pick1, pick2, pick3), (put0, put1, put2, put3)
    owned, half = pick0.shape[1], pick0.shape[2]
    block = half // 2
    slot_count = slots.shape[1]
    f32, bf16 = jnp.float32, jnp.bfloat16
    distance = place_distances(order_ref)
    member = order_ref[3]
    elements = 4
    for at, table_ref in enumerate((t0_ref, t1_ref, t2_ref, t3_ref)):
        tables[at] = table_ref[...]
    sources[...] = jnp.full(sources.shape, -1.0, f32)
    slots[...] = jnp.full(slots.shape, -1.0, f32)
    homes[...] = jnp.zeros_like(homes)
    lane_block = lax.broadcasted_iota(jnp.int32, (8, block), 1)
    rider_ids = lax.broadcasted_iota(jnp.int32, (RIDERS, owned), 0)
    for place in range(PLACES):
        riders[place] = jnp.where(
            rider_ids == place, tables[distance[place], 6:7, :], 0.0
        ).astype(bf16)
        homes[place : place + 1, :half] = tables[distance[place], 0:1, :]
        homes[place : place + 1, half:] = tables[distance[place], 1:2, :]
        for e in range(elements):
            modulus = jnp.broadcast_to(tables[distance[place], 7:8, e : e + 1], (1, block))
            factors[0, place, e : e + 1, :] = modulus
            factors[1, place, e : e + 1, :] = 1.0 / modulus

    all_homes = homes[...]
    for e in range(elements):
        shift = (all_homes.shape[1] - e * size) % all_homes.shape[1]
        moved = all_homes if e == 0 else pltpu.roll(all_homes, shift, 1)
        rows = moved[:, :block]
        rows = jnp.where((lane_block < size) & (rows < float(owned_count)), rows, -1.0)
        part, column = e // 2, (e % 2) * block
        sources[part * PLACES : (part + 1) * PLACES, column : column + block] = rows[:PLACES]

    pairs = [(a, (a + step) % PLACES) for step in (1, PLACES - 1) for a in range(PLACES)]
    for pair, (reader, owner) in enumerate(pairs):
        to_owner = pl.ds(2 + (member ^ distance[owner]), 1)
        to_reader = pl.ds(2 + (member ^ distance[reader]), 1)
        sent = tables[distance[reader], to_owner, :slot_count]
        sent = jnp.where(sent < float(local_count), sent, -1.0)
        first = float(2 * size)
        moved = sent - first + jnp.where(sent >= first + size, float(block - size), 0.0)
        slots[2 * pair : 2 * pair + 1, :] = jnp.where(sent < 0.0, -1.0, moved)
        slots[2 * pair + 1 : 2 * pair + 2, :] = tables[distance[owner], to_reader, slot_count:]
    slots_t = slots[...].T
    half_ids = lax.broadcasted_iota(jnp.int32, (LANES, half), 1).astype(f32)
    for pair in range(len(pairs)):
        found = jnp.zeros((1, half), f32)
        for start in range(0, slot_count, LANES):
            column = slots_t[start : start + LANES, 2 * pair : 2 * pair + 1]
            target = slots_t[start : start + LANES, 2 * pair + 1 : 2 * pair + 2] + 1.0
            found = found + jnp.sum(
                jnp.where(half_ids == column, target, 0.0), axis=0, keepdims=True
            )
        sources[2 * PLACES + pair : 2 * PLACES + pair + 1, :] = found - 1.0
    sources_t[...] = sources[...].T

    chunk = 256
    deep_ids = lax.broadcasted_iota(jnp.int32, (chunk, LANES), 0).astype(f32).astype(bf16)
    lane_ids = lax.broadcasted_iota(jnp.int32, (chunk, chunk), 1).astype(f32).astype(bf16)
    column_ids = lax.broadcasted_iota(jnp.int32, (chunk, LANES), 1)
    one, zero = jnp.ones((), bf16), jnp.zeros((), bf16)

    for kind, (pick, put) in enumerate(zip(picks, puts)):

        def build(place, carry):
            n = kind * PLACES + place
            source = sources[pl.ds(n, 1), :]
            for start in range(0, owned, chunk):
                moved = (source - float(start)).astype(bf16)
                for at in range(0, half, LANES):
                    wanted = jnp.broadcast_to(moved[:, at : at + LANES], (chunk, LANES))
                    pick[place, start : start + chunk, at : at + LANES] = jnp.where(
                        deep_ids == wanted, one, zero
                    )
            for start in range(0, half, chunk):
                column = jnp.sum(
                    jnp.where(column_ids == n, sources_t[start : start + chunk, :], 0.0),
                    axis=1,
                    keepdims=True,
                )
                for at in range(0, owned, chunk):
                    wanted = jnp.broadcast_to(column - float(at), (chunk, LANES)).astype(bf16)
                    wanted = jnp.concatenate([wanted] * (chunk // LANES), axis=1)
                    put[place, start : start + chunk, at : at + chunk] = jnp.where(
                        lane_ids == wanted, one, zero
                    )
            return carry

        lax.fori_loop(0, PLACES, build, 0)


def chain_kernel(
    order_ref,
    x0_ref,
    x1_ref,
    x2_ref,
    x3_ref,
    pick0,
    pick1,
    pick2,
    pick3,
    put0,
    put1,
    put2,
    put3,
    factors,
    riders,
    matrices_ref,
    own,
    values,
    terms,
    copies,
):
    owned, half = pick0.shape[1], pick0.shape[2]
    block = matrices_ref.shape[1]
    rows = own.shape[1]
    loads = rows - RIDERS
    f32, bf16 = jnp.float32, jnp.bfloat16
    distance = place_distances(order_ref)
    for at, x_ref in enumerate((x0_ref, x1_ref, x2_ref, x3_ref)):
        values[1, at, :loads, :] = x_ref[...]
    for place in range(PLACES):
        values[0, place, :loads, :] = values[1, distance[place], :loads, :]
        values[0, place, loads:, :] = jnp.zeros((RIDERS, owned), bf16)

    def multiply(left, right):
        return jnp.dot(left, right, preferred_element_type=f32)

    def beside(refs):
        return jnp.concatenate(refs, axis=1)

    def above(refs):
        return jnp.concatenate(refs, axis=0)

    def split(place, part, copied):
        copied = copied.astype(bf16)
        copies[place, 2 * part] = copied[:, :block]
        copies[place, 2 * part + 1] = copied[:, block:]

    def inner(source, place):
        split(place, 0, multiply(values[source, place], pick0[place]))

    def outer(source, place):
        ahead, behind = (place + 1) % PLACES, (place - 1) % PLACES
        fields = beside([values[source, at] for at in (place, ahead, behind)])
        split(place, 1, multiply(fields, above([pick1[place], pick2[place], pick3[place]])))

    def scaled(which, at, count):
        product = multiply(copies[at].reshape(count * 4 * rows, block), matrices_ref[which])
        scale = factors[which, at].reshape(count, 4, 1, block)
        terms[at] = (product.reshape(count, 4, rows, block) * scale).astype(bf16)

    def collect(place):
        ahead, behind = (place + 1) % PLACES, (place - 1) % PLACES
        ends = beside(
            [terms[place, e] for e in range(4)]
            + [terms[behind, 2], terms[behind, 3], terms[ahead, 2], terms[ahead, 3]]
        )
        return multiply(ends, above([put0[place], put1[place], put2[behind], put3[ahead]]))

    def stage(at, carry):
        which = lax.rem(at + 1, 2)
        source, target = lax.rem(at, 2), lax.rem(at + 1, 2)
        for place in range(PLACES):
            inner(source, place)
            outer(source, place)
        scaled(which, slice(0, PLACES), PLACES)
        for place in range(PLACES):
            summed = collect(place)
            values[target, place] = summed.astype(bf16)
            if place == 0:
                own[at] = summed

        @pl.when(at == 0)
        def _():
            for place in range(PLACES):
                values[1, place, loads:, :] = riders[place]

        return carry

    lax.fori_loop(0, 3, stage, 0)
    inner(1, 0)
    outer(1, 0)
    outer(1, 1)
    outer(1, 3)
    scaled(0, slice(0, 2), 2)
    scaled(0, slice(3, 4), 1)
    own[3] = collect(0)


def dots_kernel(
    order_ref,
    own,
    x0_ref,
    shared_ref,
    wide_ref,
    fields_ref,
    images_ref,
    gram_ref,
    inverse,
    coarse_ref,
    square,
):
    f32 = jnp.float32
    loads = fields_ref.shape[1]
    distance = place_distances(order_ref)
    devices = inverse.shape[0]
    member = order_ref[3]
    first = order_ref[4] * PLACES
    coarse_ref[...] = shared_ref[:, 0, :]
    inverse[...] = shared_ref[:, 1, :]
    square[...] = jnp.zeros_like(square)
    for place in range(PLACES):
        square[place : place + 1, :] = inverse[pl.ds(first + (member ^ distance[place]), 1), :]
    answer = jnp.dot(
        square[0:8, :devices],
        coarse_ref[...],
        precision=lax.Precision.HIGHEST,
        preferred_element_type=f32,
    )
    square[...] = jnp.zeros_like(square)
    square[0:8, :] = answer
    answer_t = square[...].T
    basis = wide_ref[0:1, :]
    start_field = own[0, :loads, :] + answer_t[:, 0:1] * basis
    start_image = own[1, :loads, :]
    next_field = own[2, :loads, :]
    next_image = own[3, :loads, :]
    for place in range(PLACES):
        column = answer_t[:, place : place + 1]
        row = loads + place
        start_image = start_image + column * own[1, row : row + 1, :]
        next_field = next_field + column * own[2, row : row + 1, :]
        next_image = next_image + column * own[3, row : row + 1, :]
    fields_ref[0] = start_field
    fields_ref[1] = next_field
    fields_ref[2] = start_image
    fields_ref[3] = next_image
    images_ref[...] = own[1, loads : loads + 8, :]
    residual = x0_ref[...].astype(f32)
    lanes = lax.broadcasted_iota(jnp.int32, square.shape, 1)
    collected = jnp.zeros(square.shape, f32)
    for at, product in enumerate(
        (
            residual * start_field,
            start_field * start_image,
            start_image * next_field,
            next_field * next_image,
            basis * start_image,
            basis * next_image,
        )
    ):
        total = jnp.sum(product, axis=1, keepdims=True)
        collected = jnp.where(lanes == at, total, collected)
    gram = collected.T[0:8, :]
    row_at = lax.broadcasted_iota(jnp.int32, gram.shape, 0)
    lane_at = lax.broadcasted_iota(jnp.int32, gram.shape, 1)
    for place in range(PLACES):
        entry = jnp.sum(
            basis * own[1, loads + place : loads + place + 1, :], axis=1, keepdims=True
        )
        here = (row_at == 6) & (lane_at == first + (member ^ distance[place]))
        gram = jnp.where(here, entry, gram)
    gram_ref[...] = jnp.broadcast_to(gram[None], gram_ref.shape)


def finish_kernel(
    order_ref,
    gram_ref,
    inverse,
    fields_ref,
    images_ref,
    wide_ref,
    padded,
    solution_hbm,
    residual_hbm,
    answer,
    square,
    iterates,
    residuals,
    sent,
):
    f32 = jnp.float32
    count = inverse.shape[0]
    owned = solution_hbm.shape[0]
    first = order_ref[4] * PLACES
    member = order_ref[3]
    distance = place_distances(order_ref)
    precise = functools.partial(
        jnp.dot, precision=lax.Precision.HIGHEST, preferred_element_type=f32
    )
    coarse = gram_ref[:, 4, :]
    answer[...] = precise(inverse[:, :count], coarse)
    answers = answer[...]
    mixed = precise(gram_ref[:, 6, :count], answers)
    sums = jnp.sum(gram_ref[...], axis=0)
    weighted, curvature = sums[0:1, :], sums[1:2, :]
    cross = sums[2:3, :] + jnp.sum(coarse * answers, axis=0, keepdims=True)
    last = sums[3:4, :] + jnp.sum(
        answers * (2.0 * gram_ref[:, 5, :] + mixed), axis=0, keepdims=True
    )
    step = weighted / curvature
    update = step * step * cross - weighted
    grown = 1.0 + update / weighted
    curvature = grown * grown * curvature - 2.0 * step * grown * cross + step * step * last
    second = update / curvature
    whole = step + second * grown
    back = step * second
    square[...] = jnp.zeros_like(square)
    square[0:1, :] = whole
    square[1:2, :] = back
    for place in range(PLACES):
        at = first + (member ^ distance[place])
        square[2 + place : 3 + place, :] = back * answer[pl.ds(at, 1), :]
    columns = square[...].T
    whole, back = columns[:, 0:1], columns[:, 1:2]
    copies = []
    for start in range(0, wide_ref.shape[1], LANES):
        part = slice(start, start + LANES)
        size = min(LANES, owned - start)
        iterate = (
            whole * fields_ref[0, :, part]
            - back * fields_ref[1, :, part]
            - columns[:, 2:3] * wide_ref[0:1, part]
        )
        change = back * fields_ref[3, :, part] - whole * fields_ref[2, :, part]
        for place in range(PLACES):
            image = images_ref[place : place + 1, part]
            change = change + columns[:, 2 + place : 3 + place] * image
        iterates[start : start + LANES, :] = iterate.T
        residuals[start : start + LANES, :] = padded[start : start + LANES, :] + change.T
        rows = slice(start, start + size)
        for at, (source, target) in enumerate(
            ((iterates, solution_hbm), (residuals, residual_hbm))
        ):
            copy = pltpu.make_async_copy(
                source.at[rows, :], target.at[rows, 0, :], sent.at[at, start // LANES]
            )
            copy.start()
            copies.append(copy)
    for copy in copies:
        copy.wait()


def slab_body(
    mesh_shape,
    forces,
    stiffness,
    local_solve,
    moduli,
    coarse_basis,
    coarse_inverse,
    send_index,
    owner_slot,
    home_slot,
):
    f32, bf16, i32 = jnp.float32, jnp.bfloat16, jnp.int32
    axes = ("sub", "grp")
    owned_count, loads = forces.shape[2:]
    size = stiffness.shape[0]
    local_count = home_slot.shape[2]
    owned_wide = round_up(owned_count, 256)
    block = round_up(size, LANES)
    half = 2 * block
    devices = mesh_shape["sub"] * mesh_shape["grp"]
    rows = loads + RIDERS
    fits = half == owned_wide and loads == LANES and moduli.shape[2] == 4
    fits = fits and send_index.shape[3] <= half // 2 and devices <= LANES
    if not fits:
        return exchange_body(
            forces,
            stiffness,
            local_solve,
            moduli,
            coarse_basis,
            coarse_inverse,
            send_index,
            owner_slot,
            home_slot,
        )
    smem = pl.BlockSpec(memory_space=pltpu.SMEM)
    vmem = pl.BlockSpec(memory_space=pltpu.VMEM)

    anywhere = pl.BlockSpec(memory_space=pltpu.HBM)
    slabs = mesh_shape["sub"]

    packed, table, shared, padded, wide, order = pl.pallas_call(
        pack_kernel,
        out_shape=(
            jax.ShapeDtypeStruct((loads, owned_wide), bf16),
            jax.ShapeDtypeStruct((8, half), f32),
            jax.ShapeDtypeStruct((devices, 2, LANES), f32),
            jax.ShapeDtypeStruct((owned_wide, loads), f32),
            jax.ShapeDtypeStruct((8, owned_wide), f32),
            jax.ShapeDtypeStruct((8,), i32),
        ),
        in_specs=[anywhere] * 7,
        out_specs=(vmem,) * 5 + (smem,),
        scratch_shapes=[
            pltpu.VMEM((1, owned_count), f32),
            pltpu.VMEM((1, devices), f32),
            pltpu.VMEM(send_index.shape[2:], i32),
            pltpu.VMEM(owner_slot.shape[2:], i32),
            pltpu.VMEM((1, local_count), i32),
            pltpu.VMEM((1, moduli.shape[2]), f32),
            pltpu.VMEM((LANES, LANES), f32),
            pltpu.SemaphoreType.DMA((7,)),
        ],
        compiler_params=pltpu.CompilerParams(vmem_limit_bytes=62 * 2**20),
        name="pack",
    )(
        forces.reshape(owned_count, 1, loads),
        coarse_basis[0],
        coarse_inverse,
        send_index[0, 0],
        owner_slot[0, 0],
        home_slot[0],
        moduli[0],
    )

    def swapped(array, distance):
        return lax.ppermute(array, "grp", [(i, i ^ distance) for i in range(PLACES)])

    near_table = swapped(table, 1)
    late, near_table = lax.optimization_barrier((packed, near_table))
    tables = [table, near_table, swapped(table, 2), swapped(table, 3)]
    fields = [packed, swapped(late, 1), swapped(packed, 2), swapped(packed, 3)]
    shared = lax.all_to_all(shared, axes, split_axis=0, concat_axis=0, tiled=True)

    widen = ((0, block - size), (0, block - size))
    matrices = jnp.stack([jnp.pad(stiffness, widen), jnp.pad(local_solve, widen)])

    *choices, factors, riders = pl.pallas_call(
        functools.partial(build_kernel, size, owned_count, local_count),
        out_shape=(
            *[jax.ShapeDtypeStruct((PLACES, owned_wide, half), bf16)] * 4,
            *[jax.ShapeDtypeStruct((PLACES, half, owned_wide), bf16)] * 4,
            jax.ShapeDtypeStruct((2, PLACES, 4, block), f32),
            jax.ShapeDtypeStruct((PLACES, RIDERS, owned_wide), bf16),
        ),
        in_specs=[smem] + [vmem] * 4,
        out_specs=(vmem,) * 10,
        scratch_shapes=[
            pltpu.VMEM((PLACES, 8, half), f32),
            pltpu.VMEM((LANES, half // 2), f32),
            pltpu.VMEM((8, 2 * half), f32),
            pltpu.VMEM((LANES, half), f32),
            pltpu.VMEM((half, LANES), f32),
        ],
        compiler_params=pltpu.CompilerParams(vmem_limit_bytes=4 * 2**20),
        cost_estimate=pl.CostEstimate(
            flops=8 * 10**9, bytes_accessed=38 * 10**6, transcendentals=0
        ),
        name="build",
    )(order, *tables)

    own = pl.pallas_call(
        chain_kernel,
        out_shape=jax.ShapeDtypeStruct((4, rows, owned_wide), f32),
        in_specs=[smem] + [vmem] * 15,
        out_specs=vmem,
        scratch_shapes=[
            pltpu.VMEM((2, PLACES, rows, owned_wide), bf16),
            pltpu.VMEM((PLACES, 4, rows, block), bf16),
            pltpu.VMEM((PLACES, 4, rows, block), bf16),
        ],
        compiler_params=pltpu.CompilerParams(vmem_limit_bytes=9 * 2**20),
        cost_estimate=pl.CostEstimate(
            flops=35 * 10**9, bytes_accessed=38 * 10**6, transcendentals=0
        ),
        name="chain",
    )(order, *fields, *choices, factors, riders, matrices)

    results, images, gram, inverse = pl.pallas_call(
        dots_kernel,
        out_shape=(
            jax.ShapeDtypeStruct((4, loads, owned_wide), f32),
            jax.ShapeDtypeStruct((8, owned_wide), f32),
            jax.ShapeDtypeStruct((devices, 8, LANES), f32),
            jax.ShapeDtypeStruct((devices, LANES), f32),
        ),
        in_specs=[smem] + [vmem] * 4,
        out_specs=(vmem,) * 4,
        scratch_shapes=[pltpu.VMEM((devices, LANES), f32), pltpu.VMEM((LANES, LANES), f32)],
        compiler_params=pltpu.CompilerParams(vmem_limit_bytes=4 * 2**20),
        name="dots",
    )(order, own, packed, shared, wide)

    gathered = lax.all_to_all(gram, axes, split_axis=0, concat_axis=0, tiled=True)
    iterate, residual = pl.pallas_call(
        finish_kernel,
        out_shape=(jax.ShapeDtypeStruct((owned_count, 1, loads), f32),) * 2,
        in_specs=[smem] + [vmem] * 6,
        out_specs=(anywhere, anywhere),
        scratch_shapes=[
            pltpu.VMEM((devices, LANES), f32),
            pltpu.VMEM((LANES, LANES), f32),
            pltpu.VMEM((owned_wide, loads), f32),
            pltpu.VMEM((owned_wide, loads), f32),
            pltpu.SemaphoreType.DMA((2, owned_wide // LANES)),
        ],
        compiler_params=pltpu.CompilerParams(vmem_limit_bytes=4 * 2**20),
        name="finish",
    )(order, gathered, inverse, results, images, wide, padded)
    return (iterate.reshape(forces.shape), residual.reshape(forces.shape))


def spread_owned(values, slot_rows):
    padded = jnp.concatenate([values, jnp.zeros((1, values.shape[1]), values.dtype)], axis=0)
    return jnp.take(padded, slot_rows, axis=0)


def element_block(copies, matrix, factors, divide):
    columns = copies.shape[-1]
    blocks = copies.reshape(factors.shape[0], matrix.shape[0], columns)
    product = jnp.einsum("ab,ebr->ear", matrix, blocks, preferred_element_type=jnp.float32)
    if divide:
        scaled = product / factors[:, None, None]
    else:
        scaled = product * factors[:, None, None]
    return scaled.astype(jnp.bfloat16).reshape(-1, columns)


def exchange_body(
    forces,
    stiffness,
    local_solve,
    moduli,
    coarse_basis,
    coarse_inverse,
    send_index,
    owner_slot,
    home_slot,
):
    loaded = forces[0, 0]
    owned_count = loaded.shape[0]
    send_rows = send_index[0, 0]
    slot_rows = owner_slot[0, 0]
    home_rows = home_slot[0, 0]
    elastic = moduli[0, 0]
    basis_values = coarse_basis[0, 0]
    groups, capacity = send_rows.shape
    block_size = stiffness.shape[0]
    inner_count = elastic.shape[0] // 2
    border_start = inner_count * block_size
    local_count = home_rows.shape[0]
    inner_elastic = elastic[:inner_count]
    outer_elastic = elastic[inner_count:]
    sent_position = (
        jnp.zeros((local_count + 1,), jnp.int32)
        .at[send_rows.reshape(-1)]
        .set(jnp.arange(groups * capacity, dtype=jnp.int32))[:local_count]
    )
    position = jnp.where(home_rows < owned_count, groups * capacity + home_rows, sent_position)
    inner_home = home_rows[:border_start]
    outer_rows = position[border_start:]
    gather_rows = jnp.concatenate([slot_rows.reshape(-1), home_rows], axis=0)
    device = lax.axis_index(("sub", "grp"))
    full_inverse = lax.all_gather(coarse_inverse, ("sub", "grp"), axis=0, tiled=True)

    def joined(received, own_values):
        columns = received.shape[2]
        return jnp.concatenate([received.reshape(-1, columns), own_values], axis=0)

    def return_terms(inner_terms, outer_copies, matrix, divide):
        outer_terms = element_block(outer_copies, matrix, outer_elastic, divide)
        element_terms = jnp.concatenate([inner_terms, outer_terms], axis=0)
        columns = element_terms.shape[1]
        padded = jnp.concatenate(
            [element_terms, jnp.zeros((1, columns), element_terms.dtype)], axis=0
        )
        outgoing = jnp.take(padded, send_rows, axis=0)
        returned = lax.all_to_all(outgoing, "grp", split_axis=0, concat_axis=0, tiled=True)
        contributions = jnp.concatenate(
            [returned.reshape(-1, columns), element_terms], axis=0
        ).astype(jnp.float32)
        summed = (
            jnp.zeros((owned_count + 1, columns), jnp.float32).at[gather_rows].add(contributions)
        )
        return summed[:owned_count]

    def residual_solve(residual):
        own_copy = residual.astype(jnp.bfloat16)
        inner_terms = element_block(
            jnp.take(own_copy, inner_home, axis=0), local_solve, inner_elastic, True
        )
        received = lax.all_to_all(
            spread_owned(own_copy, slot_rows), "grp", split_axis=0, concat_axis=0, tiled=True
        )
        outer_copies = jnp.take(joined(received, own_copy), outer_rows, axis=0)
        return return_terms(inner_terms, outer_copies, local_solve, True)

    def coarse_step(residual, local_part):
        own_term = jnp.dot(basis_values[None, :], residual, precision=lax.Precision.HIGHEST)
        spread = jnp.zeros((full_inverse.shape[0], own_term.shape[1]), jnp.float32)
        spread = lax.dynamic_update_slice(spread, own_term, (device, jnp.int32(0)))
        totals, partial_value = lax.psum(
            (spread, jnp.sum(residual * local_part, axis=0)), ("sub", "grp")
        )
        answer = jnp.dot(full_inverse, totals, precision=lax.Precision.HIGHEST)
        own_answer = lax.dynamic_slice_in_dim(answer, device, 1, 0)
        search = local_part + basis_values[:, None] * own_answer
        weighted = partial_value + jnp.sum(totals * answer, axis=0)
        return (search, weighted)

    solution = jnp.zeros_like(loaded)
    residual = loaded
    local_part = residual_solve(residual)
    search, weighted = coarse_step(residual, local_part)
    direction = search
    for iteration in range(ITERS):
        apply_own_copy = direction.astype(jnp.bfloat16)
        apply_inner_terms = element_block(
            jnp.take(apply_own_copy, inner_home, axis=0), stiffness, inner_elastic, False
        )
        apply_received = lax.all_to_all(
            spread_owned(apply_own_copy, slot_rows), "grp", split_axis=0, concat_axis=0, tiled=True
        )
        apply_outer_copies = jnp.take(joined(apply_received, apply_own_copy), outer_rows, axis=0)
        image_field = return_terms(apply_inner_terms, apply_outer_copies, stiffness, False)
        final_turn = iteration + 1 == ITERS
        curvature = lax.psum(jnp.sum(direction * image_field, axis=0), ("sub", "grp"))
        step_size = weighted / curvature
        solution = solution + step_size[None, :] * direction
        residual = residual - step_size[None, :] * image_field
        if not final_turn:
            local_part = residual_solve(residual)
            search, update = coarse_step(residual, local_part)
            direction = search + (update / weighted)[None, :] * direction
            weighted = update
    return (solution[None, None], residual[None, None])


def solution(mesh):
    if mesh.shape["grp"] == PLACES:
        body = functools.partial(slab_body, dict(mesh.shape))
    else:
        body = exchange_body
    return jax.shard_map(
        body,
        mesh=mesh,
        in_specs=(
            P("sub", "grp", None, None),
            P(),
            P(),
            P("sub", "grp", None),
            P("sub", "grp", None),
            P(("sub", "grp"), None),
            P("sub", "grp", None, None),
            P("sub", "grp", None, None),
            P("sub", "grp", None),
        ),
        out_specs=(P("sub", "grp", None, None), P("sub", "grp", None, None)),
        check_vma=False,
    )
```
